32 devices in a mesh: blk: 16 (over z, y, core), rhs: 2 (over x).
Axes of the slice: x: 2, y: 2, z: 4, core: 2. Of those that a mesh axis runs over, the one named last changes fastest.
Arguments:
- positions: float32 [3, 4096], P(None, 'blk'), may hold values from -1 to 1
- normal_angles: float32 [2, 4096], P(None, 'blk'), may hold values from -3.140625 to 3.140625
- areas: float32 [4096], P('blk'), may hold values from 1 to 6
- densities: float32 [2, 2, 4096], P('rhs', None, 'blk'), may hold values from -6 to 6
- need_owner: int32 [4096, 1], P('blk'), may hold values from 0 to 15; in each aligned block of 256 rows (0 to 255, 256 to 511, ...) at most 64 rows name the same one
- need_slot: int32 [4096], P('blk'), may hold values from 0 to 255
- near_index: int32 [32, 4096], P(None, 'blk'), may hold values from 0 to 255
- near_coef: float32 [2, 32, 4096], P(None, None, 'blk'), may hold values from -2 to 2
Outputs:
- result_field: float32 [2, 2, 4096], P('rhs', None, 'blk')
The draws below stay inside these ranges and needn't reach their ends.
Inputs may be any that keep to these rules, and one draw needn't show every extreme that they name: `need_owner`: among the 256 entries of one block of targets, at most 64 name the same owner.
All inputs are finite; a program needn't handle non-finite values.
Results may differ from the reference program's by a relative error of at most 0.0003.
Values sent between devices are 32-bit elements; how exact they have to be, the bound alone decides.
No kernel may reach another device: no remote copies, remote signals or barrier semaphores. Data moves between devices by JAX's collectives and lax.ppermute only.
A program may use at most 128 MiB of HBM per device.

```python
import math
import jax
import jax.numpy as jnp
import numpy as np
from jax import lax

P_DEV = 256
NB = 32
NEED = 256
CAP = 64
PANELS = 4096
NEEDS = 4096
N_BLK = 16


def touch_ends(drawn, stream_key, least, high):
    spot = [jax.random.randint(jax.random.fold_in(stream_key, axis), (), 0, length) for axis, length in enumerate(drawn.shape)]
    widest = drawn.shape.index(max(drawn.shape))
    beside = spot[:widest] + [(spot[widest] + 1) % drawn.shape[widest]] + spot[widest + 1:]
    return drawn.at[tuple(spot)].set(least).at[tuple(beside)].set(high)


def block_scale(rng, dims, split, smallest, largest):
    gain = 1.0
    for position, shards_of in split:
        draws = jax.random.uniform(jax.random.fold_in(jax.random.fold_in(rng, 6), position), (shards_of,), jnp.float32, smallest / len(split), largest / len(split))
        gain = gain * jnp.repeat(jnp.exp(draws), dims[position] // shards_of).reshape((-1,) + (1,) * (len(dims) - 1 - position))
    return gain


def deal_out(stream_key, own, number, rows, amount, top, bound, slope):
    sequence = jax.random.permutation(stream_key, amount)
    crowded, usual = shares(amount, rows * top, bound, slope, True), shares(amount, rows * top, bound, slope, False)
    places = jnp.arange(amount)

    def named(tallies, offset_by):
        used = int((tallies > 0).sum())
        fixed = max(1, used // 4)
        shifted = fixed + (places - fixed + offset_by * (used - fixed)) % max(1, amount - fixed)
        return jnp.zeros((amount,), jnp.int32).at[sequence[jnp.where(places < fixed, places, shifted)]].set(jnp.asarray(tallies, jnp.int32))

    tallies = jnp.where(number % 4 == 0, named(crowded, number // 4), named(usual, number - number // 4 - 1))
    mixed = jax.random.permutation(jax.random.fold_in(own, 3), amount)
    giver, sink = mixed[0:amount // 2 * 2:2], mixed[1:amount // 2 * 2:2]
    slack = jnp.minimum(tallies[giver] - 1, bound - tallies[sink]) // 2
    slack = jnp.where((giver == sequence[0]) | (sink == sequence[0]) | (tallies[sink] == 0), 0, jnp.maximum(slack, 0))
    shifted = jax.random.randint(jax.random.fold_in(own, 4), (amount // 2,), 0, 1 << 20) % (slack + 1)
    tallies = tallies.at[giver].add(-shifted).at[sink].add(shifted)
    items = jnp.searchsorted(jnp.cumsum(tallies), jnp.arange(rows * top), side="right").astype(jnp.int32)
    table = items.reshape(top, rows).T
    table = table[jax.random.permutation(jax.random.fold_in(own, 1), rows)]
    offset_by = jax.random.randint(jax.random.fold_in(own, 2), (rows, 1), 0, top)
    return jnp.take_along_axis(table, (jnp.arange(top)[None, :] + offset_by) % top, axis=1)


def shares(count, total, bound, skew, full):
    loads = [(1 << 20) // math.isqrt(rank ** skew) + 1 for rank in range(1, count + 1)]
    largest = bound if full else min(bound, max(-(-total // count), total * loads[0] // sum(loads)))
    least = 1 if total - largest >= count - 1 else 0
    given, surplus = [largest] + [least] * (count - 1), total - largest - least * (count - 1)
    while surplus > 0:
        movable = [i for i in range(1, count) if given[i] < largest] or [i for i in range(1, count) if given[i] < bound]
        whole, budget = sum([loads[i] for i in movable]), surplus
        for i in movable:
            more = min(bound - given[i], max(1, budget * loads[i] // whole), surplus)
            given[i] = given[i] + more
            surplus = surplus - more
    return np.array(given)


def centred(rng, shape, width, bound, split=(), kind=jnp.bfloat16):
    array = jax.random.normal(rng, shape, jnp.float32) * width
    if len(split) > 0:
        array = block_scale(rng, shape, split, -0.22, 0.18) * array
    return jnp.clip(array, min=-bound, max=bound).astype(kind)


def setup_inputs(seed: int = 0) -> dict:
    splits = jax.random.split(jax.random.key(seed), 9)
    positions = jnp.clip(jax.random.uniform(splits[0], (3, PANELS), jnp.float32, -1.0, 1.0) * block_scale(splits[0], (3, PANELS), ((1, 16),), -0.4, 0.0), -1.0, 1.0)
    normal_angles = jnp.clip(jax.random.uniform(splits[1], (2, PANELS), jnp.float32, -3.140625, 3.140625), -3.140625, 3.140625)
    areas = jnp.clip(jnp.exp(math.log(6.0) - 1.7917595 * jax.random.uniform(splits[2], (PANELS,), jnp.float32) ** block_scale(splits[2], (PANELS,), ((0, 16),), -0.2, 0.2)), 1.0, 6.0)
    densities = centred(splits[3], (2, 2, PANELS), 1.0, 6.0, ((0, 2), (2, 16)), jnp.float32)
    need_owner_keys = jax.random.split(jax.random.fold_in(splits[4], 1), NEEDS // NEED)
    need_owner_turns = jax.random.permutation(jax.random.fold_in(splits[4], 3), NEEDS // NEED)
    need_owner = jax.vmap(lambda own, number: deal_out(jax.random.fold_in(splits[4], 2), own, number, NEED, N_BLK, 1, CAP, 2))(need_owner_keys, need_owner_turns).reshape((NEEDS, 1))
    need_slot = touch_ends(jax.random.randint(splits[5], (NEEDS,), 0, P_DEV), jax.random.fold_in(splits[5], 1), 0, P_DEV - 1).astype(jnp.int32)
    near_index = touch_ends(jax.random.randint(splits[6], (NB, PANELS), 0, NEED), jax.random.fold_in(splits[6], 1), 0, NEED - 1).astype(jnp.int32)
    near_coef = centred(splits[7], (2, NB, PANELS), 0.15, 2.0, ((2, 16),), jnp.float32)
    return {"positions": positions, "normal_angles": normal_angles, "areas": areas, "densities": densities, "need_owner": need_owner, "need_slot": need_slot, "near_index": near_index, "near_coef": near_coef}


WAVE = 8.0
COUPLE = 1.0
SOFT = 0.1

def unit_normals(angles):
    azimuth = angles[0]
    elevation = angles[1]
    return jnp.stack([jnp.cos(azimuth) * jnp.cos(elevation), jnp.sin(azimuth) * jnp.cos(elevation), jnp.sin(elevation)], 0)

def kernel_tile(targets, geometry):
    offset_vec = targets[:, :, None] - geometry[0:3, None, :]
    distance = jnp.sqrt(lax.optimization_barrier(jnp.sum(offset_vec * offset_vec, 0)) + SOFT * SOFT)
    facing = lax.optimization_barrier(jnp.sum(offset_vec * geometry[3:6, None, :], 0))
    single = 1.0 / (4.0 * math.pi * distance)
    double = facing * single / (distance * distance)
    phases = WAVE * distance
    cosine = jnp.cos(phases)
    sines = jnp.sin(phases)
    weight = geometry[6][None, :]
    real_part = weight * (double * (cosine + phases * sines) + COUPLE * single * sines)
    imag_part = weight * (double * (sines - phases * cosine) - COUPLE * single * cosine)
    return (real_part, imag_part)

def apply_tile(targets, geometry, sources):
    real_part, imag_part = kernel_tile(targets, geometry)
    highest = lax.Precision.HIGHEST
    src_real = sources[:, 0, :]
    src_imag = sources[:, 1, :]
    out_real = jnp.einsum('ts,rs->rt', real_part, src_real, precision=highest) - jnp.einsum('ts,rs->rt', imag_part, src_imag, precision=highest)
    out_imag = jnp.einsum('ts,rs->rt', real_part, src_imag, precision=highest) + jnp.einsum('ts,rs->rt', imag_part, src_real, precision=highest)
    return (out_real, out_imag)

def reference(positions, normal_angles, areas, densities, need_owner, need_slot, near_index, near_coef):
    normals = unit_normals(normal_angles)
    weights = areas * (1.0 / math.sqrt(PANELS))
    geometry = jnp.concatenate([positions, normals, weights[None, :]], 0)
    geo_blocks = geometry.reshape(7, N_BLK, P_DEV).transpose(1, 0, 2)
    src_blocks = densities.reshape(2, 2, N_BLK, P_DEV).transpose(2, 0, 1, 3)

    def accumulate(running, block_item):
        more_real, more_imag = apply_tile(positions, block_item[0], block_item[1])
        return ((running[0] + more_real, running[1] + more_imag), None)
    zeros_init = jnp.zeros((2, PANELS), jnp.float32)
    (far_real, far_imag), _ = lax.scan(accumulate, (zeros_init, zeros_init), (geo_blocks, src_blocks))
    need_ids = need_owner[:, 0].astype(jnp.int32) * P_DEV + need_slot.astype(jnp.int32)
    device_of = jnp.arange(PANELS, dtype=jnp.int32) // P_DEV
    need_rows = device_of[None, :] * NEED + near_index.astype(jnp.int32)
    picked = densities[:, :, need_ids[need_rows]]
    coef_real = near_coef[0]
    coef_imag = near_coef[1]
    near_real = lax.optimization_barrier(jnp.sum(coef_real * picked[:, 0] - coef_imag * picked[:, 1], 1))
    near_imag = lax.optimization_barrier(jnp.sum(coef_real * picked[:, 1] + coef_imag * picked[:, 0], 1))
    field_real = 0.5 * densities[:, 0] + far_real + near_real
    field_imag = 0.5 * densities[:, 1] + far_imag + near_imag
    return jnp.stack([field_real, field_imag], 1)
```

```python
import functools
import math

import jax
import jax.numpy as jnp
from jax import lax
from jax.experimental import pallas as pl
from jax.experimental.pallas import tpu as pltpu
from jax.sharding import PartitionSpec as P

WAVE = 8.0
SOFT2 = 0.01
LANES = 128
ROWS = 8
KAPPA = WAVE / (2.0 * math.pi)

SIN7 = (4.442867755889893, -7.307443618774414, 3.594788074493408, -0.7843740582466125)
COS6 = (1.4142041206359863, -6.97764253616333, 5.715240955352783, -1.7283549308776855)
SIN11 = (
    4.442883014678955,
    -7.308249473571777,
    3.6064748764038086,
    -0.8474637866020203,
    0.1160099749663353,
    -0.009900202974677086,
)
COS10 = (
    1.4142135381698608,
    -6.9788641929626465,
    5.73988151550293,
    -1.8882750272750854,
    0.3322519063949585,
    -0.03450220078229904,
)
ATAN = (
    0.15915492177009583,
    -0.05305047705769539,
    0.031808558851480484,
    -0.02253829687833786,
    0.016709592193365097,
    -0.011514633893966675,
    0.006331379525363445,
    -0.002292047953233123,
    0.00039099997957237065,
)


def horner(z, coefs):
    acc = coefs[-1]
    for c in coefs[-2::-1]:
        acc = acc * z + c
    return acc


def sincos_turns(turns, sin_coefs, cos_coefs):
    e = turns - jnp.round(turns)
    z = e * e
    s = e * horner(z, sin_coefs)
    c = horner(z, cos_coefs)
    return s * c, 1.0 - s * s


def polar_turns(re, im):
    ax = jnp.abs(re)
    ay = jnp.abs(im)
    big = jnp.maximum(ax, ay)
    ratio = jnp.minimum(ax, ay) / jnp.where(big > 0.0, big, 1.0)
    z = ratio * ratio
    angle = ratio * horner(z, ATAN)
    angle = jnp.where(ay > ax, 0.25 - angle, angle)
    angle = jnp.where(re < 0.0, 0.5 - angle, angle)
    angle = jnp.where(im < 0.0, -angle, angle)
    return big * jnp.sqrt(1.0 + z), angle


def split3(x):
    x1 = x.astype(jnp.bfloat16).astype(jnp.float32)
    rest = x - x1
    x2 = rest.astype(jnp.bfloat16).astype(jnp.float32)
    return x1, x2, rest - x2


FEATURES = 24


def pack_body(pos_ref, ang_ref, area_ref, den_ref, out_ref):
    for h in range(pos_ref.shape[1] // LANES):
        lanes = slice(h * LANES, (h + 1) * LANES)
        base = h * ROWS
        out_ref[base : base + 3, :] = pos_ref[:, lanes]
        out_ref[base + 3 : base + 5, :] = ang_ref[:, lanes]
        out_ref[base + 5 : base + 6, :] = area_ref[:, lanes]
        out_ref[base + 6 : base + 8, :] = den_ref[:, lanes]


def field_body(
    panels_all, blocks, g_ref, owner_ref, slot_ref, index_ref, coef_ref, out_ref, feat, tgt, polar, acc
):
    width = slot_ref.shape[1]
    halves = width // LANES
    me = lax.axis_index("blk")

    def row(k):
        parts = [g_ref[pl.ds(h * ROWS + k, blocks, stride=halves * ROWS), :] for h in range(halves)]
        return jnp.concatenate(parts, 1)

    x = [row(0), row(1), row(2)]
    sa, ca = sincos_turns(row(3) * (0.5 / math.pi), SIN11, COS10)
    se, ce = sincos_turns(row(4) * (0.5 / math.pi), SIN11, COS10)
    weight = row(5) * (KAPPA / (4.0 * math.pi * math.sqrt(panels_all)))
    modulus, angle = polar_turns(row(6), row(7))
    modulus = modulus * weight
    polar[0:blocks, :] = modulus
    polar[blocks : 2 * blocks, :] = angle
    scaled = modulus * (WAVE * KAPPA)
    normal = [ca * ce * scaled, sa * ce * scaled, se * scaled]
    shift = -(x[0] * normal[0] + x[1] * normal[1] + x[2] * normal[2])
    norm2 = (x[0] * x[0] + x[1] * x[1] + x[2] * x[2]) * (KAPPA * KAPPA)

    def put(k, value):
        for h in range(halves):
            feat[pl.ds(h * 2 * FEATURES + k, blocks, stride=halves * 2 * FEATURES), :] = value[
                :, h * LANES : (h + 1) * LANES
            ]

    for c in range(3):
        y1, y2, y3 = split3(x[c] * (-2.0 * KAPPA * KAPPA))
        m1, m2, m3 = split3(normal[c])
        for base, (v1, v2, v3) in ((0, (y1, y2, y3)), (FEATURES, (m1, m2, m3))):
            put(base + c, v1)
            put(base + 3 + c, v2)
            put(base + 6 + c, v3)
            put(base + 9 + c, v1)
            put(base + 12 + c, v2)
            put(base + 15 + c, v1)
    one = jnp.ones_like(weight)
    zero = jnp.zeros_like(weight)
    n1, n2, n3 = split3(norm2 + SOFT2 * KAPPA * KAPPA)
    s1, s2, s3 = split3(shift)
    for k, v in enumerate((one, one, one, n1, n2, n3)):
        put(18 + k, v)
    for k, v in enumerate((zero, zero, zero, s1, s2, s3)):
        put(FEATURES + 18 + k, v)

    t = jnp.concatenate([g_ref[h * ROWS : h * ROWS + 3, :] for h in range(halves)], 1)
    t1, t2, t3 = split3(t)
    tt = t * t
    q1, q2, q3 = split3((tt[0:1] + tt[1:2] + tt[2:3]) * (KAPPA * KAPPA))
    ones3 = jnp.ones_like(t)
    stacked = jnp.concatenate([t1, t1, t1, t2, t2, t3, q1, q2, q3, ones3], 0)
    tgt[...] = stacked.T.astype(jnp.bfloat16)

    acc[...] = jnp.zeros_like(acc)

    @pl.loop(0, blocks)
    def _(b):
        base = b * (halves * 2 * FEATURES)
        weights = jnp.concatenate(
            [
                feat[pl.ds(pl.multiple_of(base + h * 2 * FEATURES, 8), 2 * FEATURES), :]
                for h in range(halves)
            ],
            1,
        ).astype(jnp.bfloat16)
        mod_b = polar[pl.ds(b, 1), :]
        ang_b = polar[pl.ds(blocks + b, 1), :]
        lhs = tgt[...]
        dist2 = jnp.dot(lhs, weights[0:FEATURES], preferred_element_type=jnp.float32)
        facing = jnp.dot(lhs, weights[FEATURES:], preferred_element_type=jnp.float32)
        inv = lax.rsqrt(dist2)
        s, c = sincos_turns(dist2 * inv + ang_b, SIN7, COS6)
        double = facing * (inv * inv)
        b_part = double + inv * mod_b
        a_part = double * (inv * (0.5 / math.pi))
        re = c * a_part + s * b_part
        im = s * a_part - c * b_part
        for part, value in ((0, re), (1, im)):
            total = acc[part]
            for k in range(width // LANES):
                total = total + value[:, k * LANES : (k + 1) * LANES]
            acc[part] = total

    position = owner_ref[...] ^ me
    slot = slot_ref[...]
    den = (row(6), row(7))
    need = []
    for h in range(halves):
        lanes = slice(h * LANES, (h + 1) * LANES)
        slot_h = jnp.broadcast_to(slot[:, lanes], (ROWS, LANES))
        pos_h = jnp.broadcast_to(position[:, lanes], (ROWS, LANES))
        sums = [jnp.zeros((ROWS, LANES), jnp.float32)] * 2
        for p in range(0, blocks, ROWS):
            mine = pos_h == lax.broadcasted_iota(jnp.int32, (ROWS, LANES), 0) + p
            for part in range(2):
                for k in range(halves):
                    got = jnp.take_along_axis(
                        den[part][p : p + ROWS, k * LANES : (k + 1) * LANES], slot_h % LANES, axis=1
                    )
                    sums[part] = sums[part] + jnp.where(mine & (slot_h // LANES == k), got, 0.0)
        need.append([jnp.broadcast_to(jnp.sum(v, 0, keepdims=True), (ROWS, LANES)) for v in sums])

    count = index_ref.shape[0]
    for h in range(halves):
        lanes = slice(h * LANES, (h + 1) * LANES)
        near = [jnp.zeros((ROWS, LANES), jnp.float32)] * 2
        for m in range(0, count, ROWS):
            where = index_ref[m : m + ROWS, lanes]
            picked = []
            for part in range(2):
                got = jnp.zeros((ROWS, LANES), jnp.float32)
                for k in range(halves):
                    one_half = jnp.take_along_axis(need[k][part], where % LANES, axis=1)
                    got = jnp.where(where // LANES == k, one_half, got)
                picked.append(got)
            cr = coef_ref[0, m : m + ROWS, lanes]
            ci = coef_ref[1, m : m + ROWS, lanes]
            near[0] = near[0] + (cr * picked[0] - ci * picked[1])
            near[1] = near[1] + (cr * picked[1] + ci * picked[0])
        for part in range(2):
            own = g_ref[h * ROWS + 6 + part : h * ROWS + 7 + part, :]
            far = jnp.sum(acc[part, lanes, :].T, 0, keepdims=True)
            out_ref[0, part : part + 1, lanes] = (
                0.5 * own + far + jnp.sum(near[part], 0, keepdims=True)
            )


def on_device(
    positions, normal_angles, areas, densities, need_owner, need_slot, near_index, near_coef
):
    width = positions.shape[1]
    blocks = lax.axis_size("blk")
    vmem = pl.BlockSpec(memory_space=pltpu.VMEM)
    gathered = pl.pallas_call(
        pack_body,
        out_shape=jax.ShapeDtypeStruct((ROWS * width // LANES, LANES), jnp.float32),
        in_specs=[vmem] * 4,
        out_specs=vmem,
        name="pack",
    )(positions, normal_angles, areas.reshape(1, width), densities.reshape(2, width))
    step = 1
    while step < blocks:
        other = lax.ppermute(gathered, "blk", [(i, i ^ step) for i in range(blocks)])
        gathered = jnp.concatenate([gathered, other], 0)
        step *= 2
    body = functools.partial(field_body, blocks * width, blocks)
    return pl.pallas_call(
        body,
        out_shape=jax.ShapeDtypeStruct(densities.shape, jnp.float32),
        in_specs=[vmem] * 5,
        out_specs=vmem,
        scratch_shapes=[
            pltpu.VMEM((blocks * 2 * FEATURES * width // LANES, LANES), jnp.float32),
            pltpu.VMEM((width, 3 * ROWS), jnp.bfloat16),
            pltpu.VMEM((2 * blocks, width), jnp.float32),
            pltpu.VMEM((2, width, LANES), jnp.float32),
        ],
        compiler_params=pltpu.CompilerParams(vmem_limit_bytes=32 * 1024 * 1024),
        name="field",
    )(gathered, need_owner.reshape(1, width), need_slot.reshape(1, width), near_index, near_coef)


def solution(mesh):
    in_specs = (
        P(None, "blk"),
        P(None, "blk"),
        P("blk"),
        P("rhs", None, "blk"),
        P("blk", None),
        P("blk"),
        P(None, "blk"),
        P(None, None, "blk"),
    )
    out_specs = P("rhs", None, "blk")
    return jax.shard_map(
        on_device, mesh=mesh, in_specs=in_specs, out_specs=out_specs, check_vma=False
    )
```

```python
import functools
import math

import jax
import jax.numpy as jnp
from jax import lax
from jax.experimental import pallas as pl
from jax.experimental.pallas import tpu as pltpu
from jax.sharding import PartitionSpec as P

WAVE = 8.0
SOFT2 = 0.01
LANES = 128
ROWS = 8
KAPPA = WAVE / (2.0 * math.pi)

SIN11 = (
    4.442883014678955,
    -7.308249473571777,
    3.6064748764038086,
    -0.8474637866020203,
    0.1160099749663353,
    -0.009900202974677086,
)
COS10 = (
    1.4142135381698608,
    -6.9788641929626465,
    5.73988151550293,
    -1.8882750272750854,
    0.3322519063949585,
    -0.03450220078229904,
)
ATAN = (
    0.15915492177009583,
    -0.05305047705769539,
    0.031808558851480484,
    -0.02253829687833786,
    0.016709592193365097,
    -0.011514633893966675,
    0.006331379525363445,
    -0.002292047953233123,
    0.00039099997957237065,
)


def horner(z, coefs):
    acc = coefs[-1]
    for c in coefs[-2::-1]:
        acc = acc * z + c
    return acc


def sincos_turns(turns):
    e = turns - jnp.round(turns)
    z = e * e
    s = e * horner(z, SIN11)
    c = horner(z, COS10)
    return s * c, 1.0 - s * s


def polar_turns(re, im):
    ax = jnp.abs(re)
    ay = jnp.abs(im)
    big = jnp.maximum(ax, ay)
    ratio = jnp.minimum(ax, ay) / jnp.where(big > 0.0, big, 1.0)
    z = ratio * ratio
    angle = ratio * horner(z, ATAN)
    angle = jnp.where(ay > ax, 0.25 - angle, angle)
    angle = jnp.where(re < 0.0, 0.5 - angle, angle)
    angle = jnp.where(im < 0.0, -angle, angle)
    return big * jnp.sqrt(1.0 + z), angle


def split3(x):
    x1 = x.astype(jnp.bfloat16).astype(jnp.float32)
    rest = x - x1
    x2 = rest.astype(jnp.bfloat16).astype(jnp.float32)
    return x1, x2, rest - x2


FEATURES = 24
CHUNK = 16
DEPTH = 2
UNROLL = 8
SIN5 = (1.5707885026931763, -0.6457120180130005, 0.07766739279031754)
TOP = 1.0 / SIN5[2]
SIN_A = SIN5[1] * TOP
SIN_B = SIN5[0] * TOP
TOP2 = TOP * TOP
MU = TOP2 * TOP2 / 8.0


def pack_body(pos_ref, ang_ref, area_ref, den_ref, out_ref):
    for h in range(pos_ref.shape[1] // LANES):
        lanes = slice(h * LANES, (h + 1) * LANES)
        base = h * ROWS
        out_ref[base : base + 3, :] = pos_ref[:, lanes]
        out_ref[base + 3 : base + 5, :] = ang_ref[:, lanes]
        out_ref[base + 5 : base + 6, :] = area_ref[:, lanes]
        out_ref[base + 6 : base + 8, :] = den_ref[:, lanes]


def field_body(
    panels_all, masks, g_ref, owner_ref, slot_ref, index_ref, coef_ref, out_ref, feat, tgt, polar, acc
):
    width = slot_ref.shape[1]
    halves = width // LANES
    blocks = 1 << len(masks)
    me = lax.axis_index("blk")

    def row(k):
        parts = [g_ref[pl.ds(h * ROWS + k, blocks, stride=halves * ROWS), :] for h in range(halves)]
        return jnp.concatenate(parts, 1)

    x = [row(0), row(1), row(2)]
    sa, ca = sincos_turns(row(3) * (0.5 / math.pi))
    se, ce = sincos_turns(row(4) * (0.5 / math.pi))
    weight = row(5) * (KAPPA / MU / (4.0 * math.pi * math.sqrt(panels_all)))
    modulus, angle = polar_turns(row(6), row(7))
    modulus = modulus * weight
    polar[0:blocks, :] = modulus
    polar[blocks : 2 * blocks, :] = angle
    scaled = modulus * (WAVE * KAPPA)
    normal = [ca * ce * scaled, sa * ce * scaled, se * scaled]
    shift = -(x[0] * normal[0] + x[1] * normal[1] + x[2] * normal[2])
    norm2 = (x[0] * x[0] + x[1] * x[1] + x[2] * x[2]) * (KAPPA * KAPPA)

    def put(k, value):
        for h in range(halves):
            feat[pl.ds(h * 2 * FEATURES + k, blocks, stride=halves * 2 * FEATURES), :] = value[
                :, h * LANES : (h + 1) * LANES
            ]

    for c in range(3):
        y1, y2, y3 = split3(x[c] * (-2.0 * KAPPA * KAPPA))
        m1, m2, m3 = split3(normal[c])
        for base, (v1, v2, v3) in ((0, (y1, y2, y3)), (FEATURES, (m1, m2, m3))):
            put(base + c, v1)
            put(base + 3 + c, v2)
            put(base + 6 + c, v3)
            put(base + 9 + c, v1)
            put(base + 12 + c, v2)
            put(base + 15 + c, v1)
    one = jnp.ones_like(weight)
    zero = jnp.zeros_like(weight)
    n1, n2, n3 = split3(norm2 + SOFT2 * KAPPA * KAPPA)
    s1, s2, s3 = split3(shift)
    for k, v in enumerate((one, one, one, n1, n2, n3)):
        put(18 + k, v)
    for k, v in enumerate((zero, zero, zero, s1, s2, s3)):
        put(FEATURES + 18 + k, v)

    t = jnp.concatenate([g_ref[h * ROWS : h * ROWS + 3, :] for h in range(halves)], 1)
    t1, t2, t3 = split3(t)
    tt = t * t
    q1, q2, q3 = split3((tt[0:1] + tt[1:2] + tt[2:3]) * (KAPPA * KAPPA))
    ones3 = jnp.ones_like(t)
    stacked = jnp.concatenate([t1, t1, t1, t2, t2, t3, q1, q2, q3, ones3], 0)
    tgt[...] = stacked.T.astype(jnp.bfloat16)

    acc[...] = jnp.zeros_like(acc)

    def load_weights(b):
        base = b * (halves * 2 * FEATURES)
        return jnp.concatenate(
            [
                feat[pl.ds(pl.multiple_of(base + (h * 2 + j) * FEATURES, 8), FEATURES), :]
                for j in range(2)
                for h in range(halves)
            ],
            1,
        ).astype(jnp.bfloat16)

    def products(weights, rows):
        return jnp.dot(tgt[rows, :], weights, preferred_element_type=jnp.float32)

    def add_strip(mod_b, ang_b, res, rows):
        dist2 = res[:, :width]
        facing = res[:, width:]
        inv = lax.rsqrt(dist2)
        turns = dist2 * inv + ang_b
        e = turns - jnp.round(turns)
        z = e * e
        s = ((z + SIN_A) * z + SIN_B) * e
        q = s * s
        y = TOP2 - q
        s = s * (y * lax.rsqrt(y))
        c = 0.5 * TOP2 - q
        c, s = MU - s * s, s * c
        double = facing * (inv * inv)
        b_part = double + inv * mod_b
        a_part = double * (inv * (0.5 / math.pi))
        re = c * a_part + s * b_part
        im = s * a_part - c * b_part
        for part, value in ((0, re), (1, im)):
            total = acc[part, rows, :]
            for k in range(halves):
                total = total + value[:, k * LANES : (k + 1) * LANES]
            acc[part, rows, :] = total

    spans = [slice(r, r + CHUNK) for r in range(0, width, CHUNK)]
    unroll = math.gcd(blocks, UNROLL)

    @pl.loop(0, blocks // unroll)
    def _(group):
        for u in range(unroll):
            b = group * unroll + u
            weights = load_weights(b)
            mod_b = polar[pl.ds(b, 1), :]
            ang_b = polar[pl.ds(blocks + b, 1), :]
            ready = [products(weights, rows) for rows in spans[:DEPTH]]
            for k, rows in enumerate(spans):
                if k + DEPTH < len(spans):
                    ready.append(products(weights, spans[k + DEPTH]))
                add_strip(mod_b, ang_b, ready[k], rows)

    owner = owner_ref[...]
    slot = slot_ref[...]
    den = (row(6), row(7))
    need = []
    for h in range(halves):
        lanes = slice(h * LANES, (h + 1) * LANES)
        slot_h = jnp.broadcast_to(slot[:, lanes], (ROWS, LANES))
        own_h = jnp.broadcast_to(owner[:, lanes], (ROWS, LANES))
        sums = [jnp.zeros((ROWS, LANES), jnp.float32)] * 2
        for p in range(0, blocks, ROWS):
            place = lax.broadcasted_iota(jnp.int32, (ROWS, LANES), 0) + p
            device = me
            for k, mask in enumerate(masks):
                device = device ^ (((place >> k) & 1) * mask)
            mine = own_h == device
            for part in range(2):
                for k in range(halves):
                    got = jnp.take_along_axis(
                        den[part][p : p + ROWS, k * LANES : (k + 1) * LANES], slot_h % LANES, axis=1
                    )
                    sums[part] = sums[part] + jnp.where(mine & (slot_h // LANES == k), got, 0.0)
        need.append([jnp.broadcast_to(jnp.sum(v, 0, keepdims=True), (ROWS, LANES)) for v in sums])

    count = index_ref.shape[0]
    for h in range(halves):
        lanes = slice(h * LANES, (h + 1) * LANES)
        near = [jnp.zeros((ROWS, LANES), jnp.float32)] * 2
        for m in range(0, count, ROWS):
            where = index_ref[m : m + ROWS, lanes]
            picked = []
            for part in range(2):
                got = jnp.zeros((ROWS, LANES), jnp.float32)
                for k in range(halves):
                    one_half = jnp.take_along_axis(need[k][part], where % LANES, axis=1)
                    got = jnp.where(where // LANES == k, one_half, got)
                picked.append(got)
            cr = coef_ref[0, m : m + ROWS, lanes]
            ci = coef_ref[1, m : m + ROWS, lanes]
            near[0] = near[0] + (cr * picked[0] - ci * picked[1])
            near[1] = near[1] + (cr * picked[1] + ci * picked[0])
        for part in range(2):
            own = g_ref[h * ROWS + 6 + part : h * ROWS + 7 + part, :]
            far = jnp.sum(acc[part, lanes, :].T, 0, keepdims=True)
            out_ref[0, part : part + 1, lanes] = (
                0.5 * own + far + jnp.sum(near[part], 0, keepdims=True)
            )


def on_device(
    positions, normal_angles, areas, densities, need_owner, need_slot, near_index, near_coef
):
    width = positions.shape[1]
    blocks = lax.axis_size("blk")
    vmem = pl.BlockSpec(memory_space=pltpu.VMEM)
    gathered = pl.pallas_call(
        pack_body,
        out_shape=pltpu.VMEM((ROWS * width // LANES, LANES), jnp.float32),
        in_specs=[vmem] * 4,
        out_specs=vmem,
        name="pack",
    )(positions, normal_angles, areas.reshape(1, width), densities.reshape(2, width))
    masks = []
    step = blocks // 2
    while step:
        masks.append(step | 1)
        step //= 2
    for mask in masks:
        other = lax.ppermute(gathered, "blk", [(i, i ^ mask) for i in range(blocks)])
        gathered = jnp.concatenate([gathered, other], 0)
    body = functools.partial(field_body, blocks * width, tuple(masks))
    return pl.pallas_call(
        body,
        out_shape=jax.ShapeDtypeStruct(densities.shape, jnp.float32),
        in_specs=[vmem] * 5,
        out_specs=vmem,
        scratch_shapes=[
            pltpu.VMEM((blocks * 2 * FEATURES * width // LANES, LANES), jnp.float32),
            pltpu.VMEM((width, 3 * ROWS), jnp.bfloat16),
            pltpu.VMEM((2 * blocks, width), jnp.float32),
            pltpu.VMEM((2, width, LANES), jnp.float32),
        ],
        compiler_params=pltpu.CompilerParams(vmem_limit_bytes=32 * 1024 * 1024),
        name="field",
    )(gathered, need_owner.reshape(1, width), need_slot.reshape(1, width), near_index, near_coef)


def solution(mesh):
    in_specs = (
        P(None, "blk"),
        P(None, "blk"),
        P("blk"),
        P("rhs", None, "blk"),
        P("blk", None),
        P("blk"),
        P(None, "blk"),
        P(None, None, "blk"),
    )
    out_specs = P("rhs", None, "blk")
    return jax.shard_map(
        on_device, mesh=mesh, in_specs=in_specs, out_specs=out_specs, check_vma=False
    )
```

```python
import functools
import math

import jax
import jax.numpy as jnp
from jax import lax
from jax.experimental import pallas as pl
from jax.experimental.pallas import tpu as pltpu
from jax.sharding import PartitionSpec as P

WAVE = 8.0
SOFT2 = 0.01
LANES = 128
ROWS = 8
KAPPA = WAVE / (2.0 * math.pi)

SIN11 = (
    4.442883014678955,
    -7.308249473571777,
    3.6064748764038086,
    -0.8474637866020203,
    0.1160099749663353,
    -0.009900202974677086,
)
COS10 = (
    1.4142135381698608,
    -6.9788641929626465,
    5.73988151550293,
    -1.8882750272750854,
    0.3322519063949585,
    -0.03450220078229904,
)
ATAN = (
    0.15915492177009583,
    -0.05305047705769539,
    0.031808558851480484,
    -0.02253829687833786,
    0.016709592193365097,
    -0.011514633893966675,
    0.006331379525363445,
    -0.002292047953233123,
    0.00039099997957237065,
)


def horner(z, coefs):
    acc = coefs[-1]
    for c in coefs[-2::-1]:
        acc = acc * z + c
    return acc


def sincos_turns(turns):
    e = turns - jnp.round(turns)
    z = e * e
    s = e * horner(z, SIN11)
    c = horner(z, COS10)
    return s * c, 1.0 - s * s


def polar_turns(re, im):
    ax = jnp.abs(re)
    ay = jnp.abs(im)
    big = jnp.maximum(ax, ay)
    ratio = jnp.minimum(ax, ay) / jnp.where(big > 0.0, big, 1.0)
    z = ratio * ratio
    angle = ratio * horner(z, ATAN)
    angle = jnp.where(ay > ax, 0.25 - angle, angle)
    angle = jnp.where(re < 0.0, 0.5 - angle, angle)
    angle = jnp.where(im < 0.0, -angle, angle)
    return big * jnp.sqrt(1.0 + z), angle


def split3(x):
    x1 = x.astype(jnp.bfloat16).astype(jnp.float32)
    rest = x - x1
    x2 = rest.astype(jnp.bfloat16).astype(jnp.float32)
    return x1, x2, rest - x2


FEATURES = 24
CHUNK = 16
DEPTH = 2
UNROLL = 8
SIN5 = (1.5707885026931763, -0.6457120180130005, 0.07766739279031754)
TOP = 1.0 / SIN5[2]
SIN_A = SIN5[1] * TOP
SIN_B = SIN5[0] * TOP
TOP2 = TOP * TOP
MU = TOP2 * TOP2 / 8.0


def pack_body(pos_ref, ang_ref, area_ref, den_ref, owner_ref, slot_ref, out_ref, need_ref):
    need_ref[0:1, :] = owner_ref[...]
    need_ref[1:2, :] = slot_ref[...]
    for h in range(pos_ref.shape[1] // LANES):
        lanes = slice(h * LANES, (h + 1) * LANES)
        base = h * ROWS
        out_ref[base : base + 3, :] = pos_ref[:, lanes]
        out_ref[base + 3 : base + 5, :] = ang_ref[:, lanes]
        out_ref[base + 5 : base + 6, :] = area_ref[:, lanes]
        out_ref[base + 6 : base + 8, :] = den_ref[:, lanes]


def take_row(ref, blocks, halves, k):
    parts = [ref[pl.ds(h * ROWS + k, blocks, stride=halves * ROWS), :] for h in range(halves)]
    return jnp.concatenate(parts, 1)


def source_features(panels_all, g_ref, feat, polar):
    blocks, width = polar.shape[0] // 2, polar.shape[1]
    halves = width // LANES

    def row(k):
        return take_row(g_ref, blocks, halves, k)

    x = [row(0), row(1), row(2)]
    sa, ca = sincos_turns(row(3) * (0.5 / math.pi))
    se, ce = sincos_turns(row(4) * (0.5 / math.pi))
    weight = row(5) * (KAPPA / MU / (4.0 * math.pi * math.sqrt(panels_all)))
    modulus, angle = polar_turns(row(6), row(7))
    modulus = modulus * weight
    polar[0:blocks, :] = modulus
    polar[blocks : 2 * blocks, :] = angle
    scaled = modulus * (WAVE * KAPPA)
    normal = [ca * ce * scaled, sa * ce * scaled, se * scaled]
    shift = -(x[0] * normal[0] + x[1] * normal[1] + x[2] * normal[2])
    norm2 = (x[0] * x[0] + x[1] * x[1] + x[2] * x[2]) * (KAPPA * KAPPA)

    def put(k, value):
        for h in range(halves):
            feat[pl.ds(h * 2 * FEATURES + k, blocks, stride=halves * 2 * FEATURES), :] = value[
                :, h * LANES : (h + 1) * LANES
            ]

    for c in range(3):
        y1, y2, y3 = split3(x[c] * (-2.0 * KAPPA * KAPPA))
        m1, m2, m3 = split3(normal[c])
        for base, (v1, v2, v3) in ((0, (y1, y2, y3)), (FEATURES, (m1, m2, m3))):
            put(base + c, v1)
            put(base + 3 + c, v2)
            put(base + 6 + c, v3)
            put(base + 9 + c, v1)
            put(base + 12 + c, v2)
            put(base + 15 + c, v1)
    one = jnp.ones_like(weight)
    zero = jnp.zeros_like(weight)
    n1, n2, n3 = split3(norm2 + SOFT2 * KAPPA * KAPPA)
    s1, s2, s3 = split3(shift)
    for k, v in enumerate((one, one, one, n1, n2, n3)):
        put(18 + k, v)
    for k, v in enumerate((zero, zero, zero, s1, s2, s3)):
        put(FEATURES + 18 + k, v)


def target_features(g_ref, tgt):
    halves = tgt.shape[0] // LANES
    t = jnp.concatenate([g_ref[h * ROWS : h * ROWS + 3, :] for h in range(halves)], 1)
    t1, t2, t3 = split3(t)
    tt = t * t
    q1, q2, q3 = split3((tt[0:1] + tt[1:2] + tt[2:3]) * (KAPPA * KAPPA))
    ones3 = jnp.ones_like(t)
    stacked = jnp.concatenate([t1, t1, t1, t2, t2, t3, q1, q2, q3, ones3], 0)
    tgt[...] = stacked.T.astype(jnp.bfloat16)


def add_far(feat, polar, tgt, acc):
    blocks, width = polar.shape[0] // 2, polar.shape[1]
    halves = width // LANES

    def load_weights(b):
        base = b * (halves * 2 * FEATURES)
        return jnp.concatenate(
            [
                feat[pl.ds(pl.multiple_of(base + (h * 2 + j) * FEATURES, 8), FEATURES), :]
                for j in range(2)
                for h in range(halves)
            ],
            1,
        ).astype(jnp.bfloat16)

    def products(weights, rows):
        return jnp.dot(tgt[rows, :], weights, preferred_element_type=jnp.float32)

    def add_strip(mod_b, ang_b, res, rows):
        dist2 = res[:, :width]
        facing = res[:, width:]
        inv = lax.rsqrt(dist2)
        turns = dist2 * inv + ang_b
        e = turns - jnp.round(turns)
        z = e * e
        s = ((z + SIN_A) * z + SIN_B) * e
        q = s * s
        y = TOP2 - q
        s = s * (y * lax.rsqrt(y))
        c = 0.5 * TOP2 - q
        c, s = MU - s * s, s * c
        double = facing * (inv * inv)
        b_part = double + inv * mod_b
        a_part = double * (inv * (0.5 / math.pi))
        re = c * a_part + s * b_part
        im = s * a_part - c * b_part
        for part, value in ((0, re), (1, im)):
            total = acc[part, rows, :]
            for k in range(halves):
                total = total + value[:, k * LANES : (k + 1) * LANES]
            acc[part, rows, :] = total

    spans = [slice(r, r + CHUNK) for r in range(0, width, CHUNK)]
    unroll = math.gcd(blocks, UNROLL)

    @pl.loop(0, blocks // unroll)
    def _(group):
        for u in range(unroll):
            b = group * unroll + u
            weights = load_weights(b)
            mod_b = polar[pl.ds(b, 1), :]
            ang_b = polar[pl.ds(blocks + b, 1), :]
            ready = [products(weights, rows) for rows in spans[:DEPTH]]
            for k, rows in enumerate(spans):
                if k + DEPTH < len(spans):
                    ready.append(products(weights, spans[k + DEPTH]))
                add_strip(mod_b, ang_b, ready[k], rows)


def first_body(panels_all, g_ref, acc, tgt, feat, polar):
    target_features(g_ref, tgt)
    source_features(panels_all, g_ref, feat, polar)
    acc[...] = jnp.zeros_like(acc)
    add_far(feat, polar, tgt, acc)


def more_body(panels_all, g_ref, tgt, before, acc, feat, polar):
    source_features(panels_all, g_ref, feat, polar)
    add_far(feat, polar, tgt, acc)


def last_body(
    panels_all, masks, g_ref, tgt, before, early_ref, need_ref, index_ref, coef_ref, out_ref, acc, feat, polar
):
    width = need_ref.shape[1]
    halves = width // LANES
    me = lax.axis_index("blk")
    source_features(panels_all, g_ref, feat, polar)
    add_far(feat, polar, tgt, acc)

    owner = need_ref[0:1, :]
    slot = need_ref[1:2, :]
    held = polar.shape[0] // 2
    blocks = 2 * held
    den = []
    for k in (6, 7):
        rows = [take_row(ref, held, halves, k) for ref in (early_ref, g_ref)]
        den.append(jnp.concatenate(rows, 0))
    need = []
    for h in range(halves):
        lanes = slice(h * LANES, (h + 1) * LANES)
        slot_h = jnp.broadcast_to(slot[:, lanes], (ROWS, LANES))
        own_h = jnp.broadcast_to(owner[:, lanes], (ROWS, LANES))
        sums = [jnp.zeros((ROWS, LANES), jnp.float32)] * 2
        for p in range(0, blocks, ROWS):
            place = lax.broadcasted_iota(jnp.int32, (ROWS, LANES), 0) + p
            device = me
            for k, mask in enumerate(masks):
                device = device ^ (((place >> k) & 1) * mask)
            mine = own_h == device
            for part in range(2):
                for k in range(halves):
                    got = jnp.take_along_axis(
                        den[part][p : p + ROWS, k * LANES : (k + 1) * LANES], slot_h % LANES, axis=1
                    )
                    sums[part] = sums[part] + jnp.where(mine & (slot_h // LANES == k), got, 0.0)
        need.append([jnp.broadcast_to(jnp.sum(v, 0, keepdims=True), (ROWS, LANES)) for v in sums])

    count = index_ref.shape[0]
    for h in range(halves):
        lanes = slice(h * LANES, (h + 1) * LANES)
        near = [jnp.zeros((ROWS, LANES), jnp.float32)] * 2
        for m in range(0, count, ROWS):
            where = index_ref[m : m + ROWS, lanes]
            picked = []
            for part in range(2):
                got = jnp.zeros((ROWS, LANES), jnp.float32)
                for k in range(halves):
                    one_half = jnp.take_along_axis(need[k][part], where % LANES, axis=1)
                    got = jnp.where(where // LANES == k, one_half, got)
                picked.append(got)
            cr = coef_ref[0, m : m + ROWS, lanes]
            ci = coef_ref[1, m : m + ROWS, lanes]
            near[0] = near[0] + (cr * picked[0] - ci * picked[1])
            near[1] = near[1] + (cr * picked[1] + ci * picked[0])
        for part in range(2):
            own = early_ref[h * ROWS + 6 + part : h * ROWS + 7 + part, :]
            far = jnp.sum(acc[part, lanes, :].T, 0, keepdims=True)
            out_ref[0, part : part + 1, lanes] = (
                0.5 * own + far + jnp.sum(near[part], 0, keepdims=True)
            )


def scratch(blocks, width):
    return [
        pltpu.VMEM((blocks * 2 * FEATURES * width // LANES, LANES), jnp.float32),
        pltpu.VMEM((2 * blocks, width), jnp.float32),
    ]


def far_cost(blocks, width):
    return pl.CostEstimate(
        flops=60 * blocks * width * width, bytes_accessed=0, transcendentals=2 * blocks * width * width
    )


def on_device(
    positions, normal_angles, areas, densities, need_owner, need_slot, near_index, near_coef
):
    width = positions.shape[1]
    blocks = lax.axis_size("blk")
    panels_all = blocks * width
    vmem = pl.BlockSpec(memory_space=pltpu.VMEM)
    params = pltpu.CompilerParams(vmem_limit_bytes=32 * 1024 * 1024)
    held, need = pl.pallas_call(
        pack_body,
        out_shape=(
            pltpu.VMEM((ROWS * width // LANES, LANES), jnp.float32),
            pltpu.VMEM((2, width), jnp.int32),
        ),
        in_specs=[vmem] * 6,
        out_specs=(vmem, vmem),
        name="pack",
    )(
        positions,
        normal_angles,
        areas.reshape(1, width),
        densities.reshape(2, width),
        need_owner.reshape(1, width),
        need_slot.reshape(1, width),
    )
    masks = []
    step = blocks // 2
    while step:
        masks.append(step | 1)
        step //= 2

    def trade(array, mask):
        return lax.ppermute(array, "blk", [(i, i ^ mask) for i in range(blocks)])

    acc_shape = pltpu.VMEM((2, width, LANES), jnp.float32)
    tgt_shape = pltpu.VMEM((width, FEATURES), jnp.bfloat16)
    acc = tgt = None
    count = 1
    for k, mask in enumerate(masks):
        arrived = trade(held, mask)
        early = held
        if k == 1:
            acc, tgt = pl.pallas_call(
                functools.partial(first_body, panels_all),
                out_shape=(acc_shape, tgt_shape),
                in_specs=[vmem],
                out_specs=(vmem, vmem),
                scratch_shapes=scratch(count, width),
                compiler_params=params,
                cost_estimate=far_cost(count, width),
                name="far_first",
            )(held)
        elif k > 1:
            acc = pl.pallas_call(
                functools.partial(more_body, panels_all),
                out_shape=acc_shape,
                in_specs=[vmem] * 3,
                out_specs=vmem,
                scratch_shapes=scratch(count // 2, width),
                input_output_aliases={2: 0},
                compiler_params=params,
                cost_estimate=far_cost(count // 2, width),
                name="far_more",
            )(latest, tgt, acc)
        if acc is not None:
            arrived, acc = lax.optimization_barrier((arrived, acc))
        latest = arrived
        held = jnp.concatenate([held, arrived], 0)
        count *= 2
    return pl.pallas_call(
        functools.partial(last_body, panels_all, tuple(masks)),
        out_shape=(jax.ShapeDtypeStruct(densities.shape, jnp.float32), acc_shape),
        in_specs=[vmem] * 7,
        out_specs=(vmem, vmem),
        scratch_shapes=scratch(count // 2, width),
        input_output_aliases={2: 1},
        compiler_params=params,
        cost_estimate=far_cost(count // 2, width),
        name="field",
    )(
        latest,
        tgt,
        acc,
        early,
        need,
        near_index,
        near_coef,
    )[0]


def solution(mesh):
    in_specs = (
        P(None, "blk"),
        P(None, "blk"),
        P("blk"),
        P("rhs", None, "blk"),
        P("blk", None),
        P("blk"),
        P(None, "blk"),
        P(None, None, "blk"),
    )
    out_specs = P("rhs", None, "blk")
    return jax.shard_map(
        on_device, mesh=mesh, in_specs=in_specs, out_specs=out_specs, check_vma=False
    )
```

```python
import functools
import math

import jax
import jax.numpy as jnp
from jax import lax
from jax.experimental import pallas as pl
from jax.experimental.pallas import tpu as pltpu
from jax.sharding import PartitionSpec as P

WAVE = 8.0
SOFT2 = 0.01
LANES = 128
ROWS = 8
KAPPA = WAVE / (2.0 * math.pi)

SIN11 = (
    4.442883014678955,
    -7.308249473571777,
    3.6064748764038086,
    -0.8474637866020203,
    0.1160099749663353,
    -0.009900202974677086,
)
COS10 = (
    1.4142135381698608,
    -6.9788641929626465,
    5.73988151550293,
    -1.8882750272750854,
    0.3322519063949585,
    -0.03450220078229904,
)
ATAN = (
    0.15915492177009583,
    -0.05305047705769539,
    0.031808558851480484,
    -0.02253829687833786,
    0.016709592193365097,
    -0.011514633893966675,
    0.006331379525363445,
    -0.002292047953233123,
    0.00039099997957237065,
)


def horner(z, coefs):
    acc = coefs[-1]
    for c in coefs[-2::-1]:
        acc = acc * z + c
    return acc


def sincos_turns(turns):
    e = turns - jnp.round(turns)
    z = e * e
    s = e * horner(z, SIN11)
    c = horner(z, COS10)
    return s * c, 1.0 - s * s


def polar_turns(re, im):
    ax = jnp.abs(re)
    ay = jnp.abs(im)
    big = jnp.maximum(ax, ay)
    ratio = jnp.minimum(ax, ay) / jnp.where(big > 0.0, big, 1.0)
    z = ratio * ratio
    angle = ratio * horner(z, ATAN)
    angle = jnp.where(ay > ax, 0.25 - angle, angle)
    angle = jnp.where(re < 0.0, 0.5 - angle, angle)
    angle = jnp.where(im < 0.0, -angle, angle)
    return big * jnp.sqrt(1.0 + z), angle


def split3(x):
    x1 = x.astype(jnp.bfloat16).astype(jnp.float32)
    rest = x - x1
    x2 = rest.astype(jnp.bfloat16).astype(jnp.float32)
    return x1, x2, rest - x2


FEATURES = 24
CHUNK = 16
DEPTH = 2
UNROLL = 8
SIN5 = (1.5707885026931763, -0.6457120180130005, 0.07766739279031754)
TOP = 1.0 / SIN5[2]
SIN_A = SIN5[1] * TOP
SIN_B = SIN5[0] * TOP
TOP2 = TOP * TOP
MU = TOP2 * TOP2 / 8.0


def pack_body(pos_ref, ang_ref, area_ref, den_ref, owner_ref, slot_ref, out_ref, need_ref):
    need_ref[0:1, :] = owner_ref[...]
    need_ref[1:2, :] = slot_ref[...]
    for h in range(pos_ref.shape[1] // LANES):
        lanes = slice(h * LANES, (h + 1) * LANES)
        base = h * ROWS
        out_ref[base : base + 3, :] = pos_ref[:, lanes]
        out_ref[base + 3 : base + 5, :] = ang_ref[:, lanes]
        out_ref[base + 5 : base + 6, :] = area_ref[:, lanes]
        out_ref[base + 6 : base + 8, :] = den_ref[:, lanes]


def take_row(parts, halves, k):
    step = halves * ROWS
    rows = [
        jnp.concatenate(
            [
                ref[pl.ds(first * step + h * ROWS + k, count, stride=step if count > 1 else None), :]
                for h in range(halves)
            ],
            1,
        )
        for ref, first, count in parts
    ]
    return jnp.concatenate(rows, 0)


def source_features(panels_all, parts, feat, polar):
    blocks, width = polar.shape[0] // 2, polar.shape[1]
    halves = width // LANES

    def row(k):
        return take_row(parts, halves, k)

    x = [row(0), row(1), row(2)]
    sa, ca = sincos_turns(row(3) * (0.5 / math.pi))
    se, ce = sincos_turns(row(4) * (0.5 / math.pi))
    weight = row(5) * (KAPPA / MU / (4.0 * math.pi * math.sqrt(panels_all)))
    modulus, angle = polar_turns(row(6), row(7))
    modulus = modulus * weight
    polar[0:blocks, :] = modulus
    polar[blocks : 2 * blocks, :] = angle
    scaled = modulus * (WAVE * KAPPA)
    normal = [ca * ce * scaled, sa * ce * scaled, se * scaled]
    shift = -(x[0] * normal[0] + x[1] * normal[1] + x[2] * normal[2])
    norm2 = (x[0] * x[0] + x[1] * x[1] + x[2] * x[2]) * (KAPPA * KAPPA)

    def put(k, value):
        stride = halves * 2 * FEATURES if blocks > 1 else None
        for h in range(halves):
            feat[pl.ds(h * 2 * FEATURES + k, blocks, stride=stride), :] = value[
                :, h * LANES : (h + 1) * LANES
            ]

    for c in range(3):
        y1, y2, y3 = split3(x[c] * (-2.0 * KAPPA * KAPPA))
        m1, m2, m3 = split3(normal[c])
        for base, (v1, v2, v3) in ((0, (y1, y2, y3)), (FEATURES, (m1, m2, m3))):
            put(base + c, v1)
            put(base + 3 + c, v2)
            put(base + 6 + c, v3)
            put(base + 9 + c, v1)
            put(base + 12 + c, v2)
            put(base + 15 + c, v1)
    one = jnp.ones_like(weight)
    zero = jnp.zeros_like(weight)
    n1, n2, n3 = split3(norm2 + SOFT2 * KAPPA * KAPPA)
    s1, s2, s3 = split3(shift)
    for k, v in enumerate((one, one, one, n1, n2, n3)):
        put(18 + k, v)
    for k, v in enumerate((zero, zero, zero, s1, s2, s3)):
        put(FEATURES + 18 + k, v)


def target_features(g_ref, tgt, first):
    halves = tgt.shape[0] // 2 // LANES
    width = halves * LANES
    t = jnp.concatenate([g_ref[h * ROWS : h * ROWS + 3, :] for h in range(halves)], 1)
    t1, t2, t3 = split3(t)
    tt = t * t
    q1, q2, q3 = split3((tt[0:1] + tt[1:2] + tt[2:3]) * (KAPPA * KAPPA))
    ones3 = jnp.ones_like(t)
    stacked = jnp.concatenate([t1, t1, t1, t2, t2, t3, q1, q2, q3, ones3], 0)
    tgt[first : first + width, :] = stacked.T.astype(jnp.bfloat16)


def add_far(feat, polar, tgt, acc, first_block, count, top, bottom):
    blocks, width = polar.shape[0] // 2, polar.shape[1]
    halves = width // LANES

    def load_weights(b):
        base = b * (halves * 2 * FEATURES)
        return jnp.concatenate(
            [
                feat[pl.ds(pl.multiple_of(base + (h * 2 + j) * FEATURES, 8), FEATURES), :]
                for j in range(2)
                for h in range(halves)
            ],
            1,
        ).astype(jnp.bfloat16)

    def products(weights, rows):
        return jnp.dot(tgt[rows, :], weights, preferred_element_type=jnp.float32)

    def add_strip(mod_b, ang_b, res, rows):
        dist2 = res[:, :width]
        facing = res[:, width:]
        inv = lax.rsqrt(dist2)
        turns = dist2 * inv + ang_b
        e = turns - jnp.round(turns)
        z = e * e
        s = ((z + SIN_A) * z + SIN_B) * e
        q = s * s
        y = TOP2 - q
        s = s * (y * lax.rsqrt(y))
        c = 0.5 * TOP2 - q
        c, s = MU - s * s, s * c
        double = facing * (inv * inv)
        b_part = double + inv * mod_b
        a_part = double * (inv * (0.5 / math.pi))
        re = c * a_part + s * b_part
        im = s * a_part - c * b_part
        for part, value in ((0, re), (1, im)):
            total = acc[part, rows, :]
            for k in range(halves):
                total = total + value[:, k * LANES : (k + 1) * LANES]
            acc[part, rows, :] = total

    spans = [slice(r, r + CHUNK) for r in range(top, bottom, CHUNK)]
    unroll = math.gcd(count, UNROLL * width // (bottom - top))

    @pl.loop(0, count // unroll)
    def _(group):
        for u in range(unroll):
            b = first_block + group * unroll + u
            weights = load_weights(b)
            mod_b = polar[pl.ds(b, 1), :]
            ang_b = polar[pl.ds(blocks + b, 1), :]
            ready = [products(weights, rows) for rows in spans[:DEPTH]]
            for k, rows in enumerate(spans):
                if k + DEPTH < len(spans):
                    ready.append(products(weights, spans[k + DEPTH]))
                add_strip(mod_b, ang_b, ready[k], rows)


def far_sums(acc, first, width):
    return [
        jnp.concatenate(
            [
                jnp.sum(acc[part, h : h + LANES, :].T, 0, keepdims=True)
                for h in range(first, first + width, LANES)
            ],
            1,
        )
        for part in range(2)
    ]


def own_body(panels_all, own_ref, index_in, coef_in, acc, tgt, index_out, coef_out, feat, polar, sems):
    width = polar.shape[1]
    copies = [
        pltpu.make_async_copy(index_in, index_out, sems.at[0]),
        pltpu.make_async_copy(coef_in, coef_out, sems.at[1]),
    ]
    for copy in copies:
        copy.start()
    target_features(own_ref, tgt, 0)
    source_features(panels_all, [(own_ref, 0, 1)], feat, polar)
    acc[...] = jnp.zeros_like(acc)
    add_far(feat, polar, tgt, acc, 0, 1, 0, width)
    for copy in copies:
        copy.wait()


def mate_body(panels_all, own_ref, mate_ref, g_ref, acc_in, tgt_in, acc, tgt, feat, polar):
    width = polar.shape[1]
    target_features(mate_ref, tgt, width)
    source_features(panels_all, [(own_ref, 0, 1), (g_ref, 0, 1)], feat, polar)
    add_far(feat, polar, tgt, acc, 0, 1, width, 2 * width)
    add_far(feat, polar, tgt, acc, 1, 1, 0, 2 * width)


def both_body(panels_all, final, g_ref, tgt, acc_in, acc, *rest):
    feat, polar = rest[-2:]
    blocks, width = polar.shape[0] // 2, polar.shape[1]
    source_features(panels_all, [(g_ref, 0, blocks)], feat, polar)
    add_far(feat, polar, tgt, acc, 0, blocks, 0, 2 * width)
    if final:
        gift = rest[0]
        gift[...] = jnp.zeros_like(gift)
        sums = far_sums(acc, width, width)
        for part in range(2):
            for h in range(width // LANES):
                k = part * (width // LANES) + h
                gift[k : k + 1, :] = sums[part][:, h * LANES : (h + 1) * LANES]


def self_body(panels_all, g_ref, tgt, acc_in, acc, feat, polar):
    blocks, width = polar.shape[0] // 2, polar.shape[1]
    source_features(panels_all, [(g_ref, 0, blocks)], feat, polar)
    add_far(feat, polar, tgt, acc, 0, blocks, 0, width)


def last_body(
    panels_all, masks, g_ref, tgt, acc_in, early_ref, need_ref, index_ref, coef_ref, out_ref, acc, feat, polar
):
    width = need_ref.shape[1]
    halves = width // LANES
    me = lax.axis_index("blk")
    fresh = polar.shape[0] // 2
    held = 2 * fresh
    source_features(panels_all, [(g_ref, fresh, fresh)], feat, polar)
    add_far(feat, polar, tgt, acc, 0, fresh, 0, width)
    far = far_sums(acc, 0, width)

    owner = need_ref[0:1, :]
    slot = need_ref[1:2, :]
    blocks = 2 * held
    den = []
    for k in (6, 7):
        den.append(take_row([(early_ref, 0, held), (g_ref, 0, held)], halves, k))
    need = []
    for h in range(halves):
        lanes = slice(h * LANES, (h + 1) * LANES)
        slot_h = jnp.broadcast_to(slot[:, lanes], (ROWS, LANES))
        own_h = jnp.broadcast_to(owner[:, lanes], (ROWS, LANES))
        sums = [jnp.zeros((ROWS, LANES), jnp.float32)] * 2
        for p in range(0, blocks, ROWS):
            place = lax.broadcasted_iota(jnp.int32, (ROWS, LANES), 0) + p
            device = me
            for k, mask in enumerate(masks):
                device = device ^ (((place >> k) & 1) * mask)
            mine = own_h == device
            for part in range(2):
                for k in range(halves):
                    got = jnp.take_along_axis(
                        den[part][p : p + ROWS, k * LANES : (k + 1) * LANES], slot_h % LANES, axis=1
                    )
                    sums[part] = sums[part] + jnp.where(mine & (slot_h // LANES == k), got, 0.0)
        need.append([jnp.broadcast_to(jnp.sum(v, 0, keepdims=True), (ROWS, LANES)) for v in sums])

    count = index_ref.shape[0]
    for h in range(halves):
        lanes = slice(h * LANES, (h + 1) * LANES)
        near = [jnp.zeros((ROWS, LANES), jnp.float32)] * 2
        for m in range(0, count, ROWS):
            where = index_ref[m : m + ROWS, lanes]
            picked = []
            for part in range(2):
                got = jnp.zeros((ROWS, LANES), jnp.float32)
                for k in range(halves):
                    one_half = jnp.take_along_axis(need[k][part], where % LANES, axis=1)
                    got = jnp.where(where // LANES == k, one_half, got)
                picked.append(got)
            cr = coef_ref[0, m : m + ROWS, lanes]
            ci = coef_ref[1, m : m + ROWS, lanes]
            near[0] = near[0] + (cr * picked[0] - ci * picked[1])
            near[1] = near[1] + (cr * picked[1] + ci * picked[0])
        for part in range(2):
            own = early_ref[h * ROWS + 6 + part : h * ROWS + 7 + part, :]
            k = blocks * halves * ROWS // 2 + part * halves + h
            gift = g_ref[k : k + 1, :]
            out_ref[0, part : part + 1, lanes] = (
                0.5 * own + (far[part][:, lanes] + gift) + jnp.sum(near[part], 0, keepdims=True)
            )


def scratch(blocks, width):
    return [
        pltpu.VMEM((blocks * 2 * FEATURES * width // LANES, LANES), jnp.float32),
        pltpu.VMEM((2 * blocks, width), jnp.float32),
    ]


def far_cost(blocks, width):
    return pl.CostEstimate(
        flops=60 * blocks * width * width, bytes_accessed=0, transcendentals=2 * blocks * width * width
    )


def on_device(
    positions, normal_angles, areas, densities, need_owner, need_slot, near_index, near_coef
):
    width = positions.shape[1]
    blocks = lax.axis_size("blk")
    panels_all = blocks * width
    vmem = pl.BlockSpec(memory_space=pltpu.VMEM)
    params = pltpu.CompilerParams(vmem_limit_bytes=32 * 1024 * 1024)
    held, need = pl.pallas_call(
        pack_body,
        out_shape=(
            pltpu.VMEM((ROWS * width // LANES, LANES), jnp.float32),
            pltpu.VMEM((2, width), jnp.int32),
        ),
        in_specs=[vmem] * 6,
        out_specs=(vmem, vmem),
        name="pack",
    )(
        positions,
        normal_angles,
        areas.reshape(1, width),
        densities.reshape(2, width),
        need_owner.reshape(1, width),
        need_slot.reshape(1, width),
    )
    masks = []
    step = blocks // 2
    while step:
        masks.append(step | 1)
        step //= 2

    def trade(array, mask):
        return lax.ppermute(array, "blk", [(i, i ^ mask) for i in range(blocks)])

    def kernel(body, out_shape, operands, work, blocks_in, aliases=None):
        several = isinstance(out_shape, tuple)
        return pl.pallas_call(
            body,
            out_shape=out_shape,
            in_specs=[vmem] * len(operands),
            out_specs=(vmem,) * len(out_shape) if several else vmem,
            scratch_shapes=scratch(blocks_in, width),
            input_output_aliases=aliases or {},
            compiler_params=params,
            cost_estimate=far_cost(work, width),
            name="far",
        )(*operands)

    acc_shape = pltpu.VMEM((2, 2 * width, LANES), jnp.float32)
    tgt_shape = pltpu.VMEM((2 * width, FEATURES), jnp.bfloat16)
    gift_shape = pltpu.VMEM((ROWS, LANES), jnp.float32)
    own = latest = held
    early = mate = acc = tgt = gift = None
    count = 1
    for k, mask in enumerate(masks):
        early = held
        send = held if gift is None else jnp.concatenate([held, gift], 0)
        send, latest = lax.optimization_barrier((send, latest))
        arrived = trade(send, mask)
        if k == 0:
            acc, tgt, index, coef = pl.pallas_call(
                functools.partial(own_body, panels_all),
                out_shape=(
                    acc_shape,
                    tgt_shape,
                    pltpu.VMEM(near_index.shape, near_index.dtype),
                    pltpu.VMEM(near_coef.shape, near_coef.dtype),
                ),
                in_specs=[vmem, pl.BlockSpec(memory_space=pltpu.HBM), pl.BlockSpec(memory_space=pltpu.HBM)],
                out_specs=(vmem,) * 4,
                scratch_shapes=scratch(1, width) + [pltpu.SemaphoreType.DMA((2,))],
                compiler_params=params,
                cost_estimate=far_cost(1, width),
                name="far",
            )(
                own,
                pltpu.with_memory_space_constraint(near_index, pltpu.HBM),
                pltpu.with_memory_space_constraint(near_coef, pltpu.HBM),
            )
            own, acc = lax.optimization_barrier((own, acc))
            mate = trade(own, 1)
        elif k == 1:
            acc, tgt = kernel(
                functools.partial(mate_body, panels_all),
                (acc_shape, tgt_shape),
                (own, mate, latest, acc, tgt),
                3,
                2,
                {3: 0, 4: 1},
            )
        elif k < len(masks) - 1:
            final = k == len(masks) - 2
            out = kernel(
                functools.partial(both_body, panels_all, final),
                (acc_shape, gift_shape) if final else (acc_shape,),
                (latest, tgt, acc),
                count,
                count // 2,
                {2: 0},
            )
            acc = out[0]
            gift = out[1] if final else None
        else:
            acc = kernel(
                functools.partial(self_body, panels_all), acc_shape, (latest, tgt, acc), count // 2, count // 2, {2: 0}
            )
        arrived, acc = lax.optimization_barrier((arrived, acc))
        latest = arrived
        held = jnp.concatenate([held, arrived], 0)
        count *= 2
    out = kernel(
        functools.partial(last_body, panels_all, tuple(masks)),
        (jax.ShapeDtypeStruct(densities.shape, jnp.float32), acc_shape),
        (latest, tgt, acc, early, need, index, coef),
        count // 4,
        count // 4,
        {2: 1},
    )
    return out[0]


def solution(mesh):
    in_specs = (
        P(None, "blk"),
        P(None, "blk"),
        P("blk"),
        P("rhs", None, "blk"),
        P("blk", None),
        P("blk"),
        P(None, "blk"),
        P(None, None, "blk"),
    )
    out_specs = P("rhs", None, "blk")
    return jax.shard_map(
        on_device, mesh=mesh, in_specs=in_specs, out_specs=out_specs, check_vma=False
    )
```

```python
import functools
import math

import jax
import jax.numpy as jnp
from jax import lax
from jax.experimental import pallas as pl
from jax.experimental.pallas import tpu as pltpu
from jax.sharding import PartitionSpec as P

WAVE = 8.0
SOFT2 = 0.01
LANES = 128
ROWS = 8
KAPPA = WAVE / (2.0 * math.pi)

SIN11 = (
    4.442883014678955,
    -7.308249473571777,
    3.6064748764038086,
    -0.8474637866020203,
    0.1160099749663353,
    -0.009900202974677086,
)
COS10 = (
    1.4142135381698608,
    -6.9788641929626465,
    5.73988151550293,
    -1.8882750272750854,
    0.3322519063949585,
    -0.03450220078229904,
)
ATAN = (
    0.15915492177009583,
    -0.05305047705769539,
    0.031808558851480484,
    -0.02253829687833786,
    0.016709592193365097,
    -0.011514633893966675,
    0.006331379525363445,
    -0.002292047953233123,
    0.00039099997957237065,
)


def horner(z, coefs):
    acc = coefs[-1]
    for c in coefs[-2::-1]:
        acc = acc * z + c
    return acc


def sincos_turns(turns):
    e = turns - jnp.round(turns)
    z = e * e
    s = e * horner(z, SIN11)
    c = horner(z, COS10)
    return s * c, 1.0 - s * s


def polar_turns(re, im):
    ax = jnp.abs(re)
    ay = jnp.abs(im)
    big = jnp.maximum(ax, ay)
    ratio = jnp.minimum(ax, ay) / jnp.where(big > 0.0, big, 1.0)
    z = ratio * ratio
    angle = ratio * horner(z, ATAN)
    angle = jnp.where(ay > ax, 0.25 - angle, angle)
    angle = jnp.where(re < 0.0, 0.5 - angle, angle)
    angle = jnp.where(im < 0.0, -angle, angle)
    return big * jnp.sqrt(1.0 + z), angle


def split3(x):
    x1 = x.astype(jnp.bfloat16).astype(jnp.float32)
    rest = x - x1
    x2 = rest.astype(jnp.bfloat16).astype(jnp.float32)
    return x1, x2, rest - x2


FEATURES = 24
CHUNK = 16
DEPTH = 2
UNROLL = 8
SIN5 = (2.0943219661712646, -1.5290753841400146, 0.32005560398101807)
TOP = 1.0 / SIN5[2]
SIN_A = SIN5[1] * TOP
SIN_B = SIN5[0] * TOP
TOP2 = TOP * TOP
MU = TOP2 * TOP / 4.0


def pack_body(pos_ref, ang_ref, area_ref, den_ref, owner_ref, slot_ref, out_ref, need_ref):
    need_ref[0:1, :] = owner_ref[...]
    need_ref[1:2, :] = slot_ref[...]
    for h in range(pos_ref.shape[1] // LANES):
        lanes = slice(h * LANES, (h + 1) * LANES)
        base = h * ROWS
        out_ref[base : base + 3, :] = pos_ref[:, lanes]
        out_ref[base + 3 : base + 5, :] = ang_ref[:, lanes]
        out_ref[base + 5 : base + 6, :] = area_ref[:, lanes]
        out_ref[base + 6 : base + 8, :] = den_ref[:, lanes]


def take_row(parts, halves, k):
    step = halves * ROWS
    rows = [
        jnp.concatenate(
            [
                ref[pl.ds(first * step + h * ROWS + k, count, stride=step if count > 1 else None), :]
                for h in range(halves)
            ],
            1,
        )
        for ref, first, count in parts
    ]
    return jnp.concatenate(rows, 0)


def source_features(panels_all, parts, feat, polar):
    blocks, width = polar.shape[0] // 2, polar.shape[1]
    halves = width // LANES

    def row(k):
        return take_row(parts, halves, k)

    x = [row(0), row(1), row(2)]
    sa, ca = sincos_turns(row(3) * (0.5 / math.pi))
    se, ce = sincos_turns(row(4) * (0.5 / math.pi))
    weight = row(5) * (KAPPA / MU / (4.0 * math.pi * math.sqrt(panels_all)))
    modulus, angle = polar_turns(row(6), row(7))
    modulus = modulus * weight
    polar[0:blocks, :] = modulus
    polar[blocks : 2 * blocks, :] = angle
    scaled = modulus * (WAVE * KAPPA)
    normal = [ca * ce * scaled, sa * ce * scaled, se * scaled]
    shift = -(x[0] * normal[0] + x[1] * normal[1] + x[2] * normal[2])
    norm2 = (x[0] * x[0] + x[1] * x[1] + x[2] * x[2]) * (KAPPA * KAPPA)

    def put(k, value):
        stride = halves * 2 * FEATURES if blocks > 1 else None
        for h in range(halves):
            feat[pl.ds(h * 2 * FEATURES + k, blocks, stride=stride), :] = value[
                :, h * LANES : (h + 1) * LANES
            ]

    for c in range(3):
        y1, y2, y3 = split3(x[c] * (-2.0 * KAPPA * KAPPA))
        m1, m2, m3 = split3(normal[c])
        for base, (v1, v2, v3) in ((0, (y1, y2, y3)), (FEATURES, (m1, m2, m3))):
            put(base + c, v1)
            put(base + 3 + c, v2)
            put(base + 6 + c, v3)
            put(base + 9 + c, v1)
            put(base + 12 + c, v2)
            put(base + 15 + c, v1)
    one = jnp.ones_like(weight)
    zero = jnp.zeros_like(weight)
    n1, n2, n3 = split3(norm2 + SOFT2 * KAPPA * KAPPA)
    s1, s2, s3 = split3(shift)
    for k, v in enumerate((one, one, one, n1, n2, n3)):
        put(18 + k, v)
    for k, v in enumerate((zero, zero, zero, s1, s2, s3)):
        put(FEATURES + 18 + k, v)


def target_features(g_ref, tgt, first):
    halves = tgt.shape[0] // 2 // LANES
    width = halves * LANES
    t = jnp.concatenate([g_ref[h * ROWS : h * ROWS + 3, :] for h in range(halves)], 1)
    t1, t2, t3 = split3(t)
    tt = t * t
    q1, q2, q3 = split3((tt[0:1] + tt[1:2] + tt[2:3]) * (KAPPA * KAPPA))
    ones3 = jnp.ones_like(t)
    stacked = jnp.concatenate([t1, t1, t1, t2, t2, t3, q1, q2, q3, ones3], 0)
    tgt[first : first + width, :] = stacked.T.astype(jnp.bfloat16)


def add_far(feat, polar, tgt, acc, first_block, count, top, bottom):
    blocks, width = polar.shape[0] // 2, polar.shape[1]
    halves = width // LANES

    def load_weights(b):
        base = b * (halves * 2 * FEATURES)
        return jnp.concatenate(
            [
                feat[pl.ds(pl.multiple_of(base + (h * 2 + j) * FEATURES, 8), FEATURES), :]
                for j in range(2)
                for h in range(halves)
            ],
            1,
        ).astype(jnp.bfloat16)

    def products(weights, rows):
        return jnp.dot(tgt[rows, :], weights, preferred_element_type=jnp.float32)

    def add_strip(mod_b, ang_b, res, rows):
        dist2 = res[:, :width]
        facing = res[:, width:]
        inv = lax.rsqrt(dist2)
        turns = dist2 * inv + ang_b
        e = turns - jnp.round(turns)
        z = e * e
        s = ((z + SIN_A) * z + SIN_B) * e
        q = s * s
        y = TOP2 - q
        c = (y * lax.rsqrt(y)) * (0.25 * TOP2 - q)
        s = s * (0.75 * TOP2 - q)
        double = facing * (inv * inv)
        b_part = double + inv * mod_b
        a_part = double * (inv * (0.5 / math.pi))
        re = c * a_part + s * b_part
        im = s * a_part - c * b_part
        for part, value in ((0, re), (1, im)):
            total = acc[part, rows, :]
            for k in range(halves):
                total = total + value[:, k * LANES : (k + 1) * LANES]
            acc[part, rows, :] = total

    spans = [slice(r, r + CHUNK) for r in range(top, bottom, CHUNK)]
    unroll = math.gcd(count, UNROLL * width // (bottom - top))

    def add_block(b):
        weights = load_weights(b)
        mod_b = polar[pl.ds(b, 1), :]
        ang_b = polar[pl.ds(blocks + b, 1), :]
        ready = [products(weights, rows) for rows in spans[:DEPTH]]
        for k, rows in enumerate(spans):
            if k + DEPTH < len(spans):
                ready.append(products(weights, spans[k + DEPTH]))
            add_strip(mod_b, ang_b, ready[k], rows)

    if count == unroll:
        for u in range(count):
            add_block(first_block + u)
    else:

        @pl.loop(0, count // unroll)
        def _(group):
            for u in range(unroll):
                add_block(first_block + group * unroll + u)


def far_sums(acc, first, width):
    return [
        jnp.concatenate(
            [
                jnp.sum(acc[part, h : h + LANES, :].T, 0, keepdims=True)
                for h in range(first, first + width, LANES)
            ],
            1,
        )
        for part in range(2)
    ]


def own_body(panels_all, own_ref, index_in, coef_in, acc, tgt, index_out, coef_out, feat, polar, sems):
    width = polar.shape[1]
    copies = [
        pltpu.make_async_copy(index_in, index_out, sems.at[0]),
        pltpu.make_async_copy(coef_in, coef_out, sems.at[1]),
    ]
    for copy in copies:
        copy.start()
    target_features(own_ref, tgt, 0)
    source_features(panels_all, [(own_ref, 0, 1)], feat, polar)
    acc[...] = jnp.zeros_like(acc)
    add_far(feat, polar, tgt, acc, 0, 1, 0, width)
    for copy in copies:
        copy.wait()


def mate_body(panels_all, own_ref, mate_ref, g_ref, acc_in, tgt_in, acc, tgt, feat, polar):
    width = polar.shape[1]
    target_features(mate_ref, tgt, width)
    source_features(panels_all, [(own_ref, 0, 1), (g_ref, 0, 1)], feat, polar)
    add_far(feat, polar, tgt, acc, 0, 1, width, 2 * width)
    add_far(feat, polar, tgt, acc, 1, 1, 0, 2 * width)


def both_body(panels_all, final, g_ref, tgt, acc_in, acc, *rest):
    feat, polar = rest[-2:]
    blocks, width = polar.shape[0] // 2, polar.shape[1]
    source_features(panels_all, [(g_ref, 0, blocks)], feat, polar)
    add_far(feat, polar, tgt, acc, 0, blocks, 0, 2 * width)
    if final:
        gift = rest[0]
        gift[...] = jnp.zeros_like(gift)
        sums = far_sums(acc, width, width)
        for part in range(2):
            for h in range(width // LANES):
                k = part * (width // LANES) + h
                gift[k : k + 1, :] = sums[part][:, h * LANES : (h + 1) * LANES]


def self_body(panels_all, g_ref, tgt, acc_in, acc, feat, polar):
    blocks, width = polar.shape[0] // 2, polar.shape[1]
    source_features(panels_all, [(g_ref, 0, blocks)], feat, polar)
    add_far(feat, polar, tgt, acc, 0, blocks, 0, width)


def last_body(
    panels_all, masks, g_ref, tgt, acc_in, early_ref, need_ref, index_ref, coef_ref, out_ref, acc, feat, polar
):
    width = need_ref.shape[1]
    halves = width // LANES
    me = lax.axis_index("blk")
    fresh = polar.shape[0] // 2
    held = 2 * fresh
    source_features(panels_all, [(g_ref, fresh, fresh)], feat, polar)
    add_far(feat, polar, tgt, acc, 0, fresh, 0, width)
    far = far_sums(acc, 0, width)

    owner = need_ref[0:1, :]
    slot = need_ref[1:2, :]
    blocks = 2 * held
    den = []
    for k in (6, 7):
        den.append(take_row([(early_ref, 0, held), (g_ref, 0, held)], halves, k))
    need = []
    for h in range(halves):
        lanes = slice(h * LANES, (h + 1) * LANES)
        slot_h = jnp.broadcast_to(slot[:, lanes], (ROWS, LANES))
        own_h = jnp.broadcast_to(owner[:, lanes], (ROWS, LANES))
        sums = [jnp.zeros((ROWS, LANES), jnp.float32)] * 2
        for p in range(0, blocks, ROWS):
            place = lax.broadcasted_iota(jnp.int32, (ROWS, LANES), 0) + p
            device = me
            for k, mask in enumerate(masks):
                device = device ^ (((place >> k) & 1) * mask)
            mine = own_h == device
            for part in range(2):
                for k in range(halves):
                    got = jnp.take_along_axis(
                        den[part][p : p + ROWS, k * LANES : (k + 1) * LANES], slot_h % LANES, axis=1
                    )
                    sums[part] = sums[part] + jnp.where(mine & (slot_h // LANES == k), got, 0.0)
        need.append([jnp.broadcast_to(jnp.sum(v, 0, keepdims=True), (ROWS, LANES)) for v in sums])

    count = index_ref.shape[0]
    for h in range(halves):
        lanes = slice(h * LANES, (h + 1) * LANES)
        near = [jnp.zeros((ROWS, LANES), jnp.float32)] * 2
        for m in range(0, count, ROWS):
            where = index_ref[m : m + ROWS, lanes]
            picked = []
            for part in range(2):
                got = jnp.zeros((ROWS, LANES), jnp.float32)
                for k in range(halves):
                    one_half = jnp.take_along_axis(need[k][part], where % LANES, axis=1)
                    got = jnp.where(where // LANES == k, one_half, got)
                picked.append(got)
            cr = coef_ref[0, m : m + ROWS, lanes]
            ci = coef_ref[1, m : m + ROWS, lanes]
            near[0] = near[0] + (cr * picked[0] - ci * picked[1])
            near[1] = near[1] + (cr * picked[1] + ci * picked[0])
        for part in range(2):
            own = early_ref[h * ROWS + 6 + part : h * ROWS + 7 + part, :]
            k = blocks * halves * ROWS // 2 + part * halves + h
            gift = g_ref[k : k + 1, :]
            out_ref[0, part : part + 1, lanes] = (
                0.5 * own + (far[part][:, lanes] + gift) + jnp.sum(near[part], 0, keepdims=True)
            )


def scratch(blocks, width):
    return [
        pltpu.VMEM((blocks * 2 * FEATURES * width // LANES, LANES), jnp.float32),
        pltpu.VMEM((2 * blocks, width), jnp.float32),
    ]


def far_cost(blocks, width):
    return pl.CostEstimate(
        flops=60 * blocks * width * width, bytes_accessed=0, transcendentals=2 * blocks * width * width
    )


def on_device(
    positions, normal_angles, areas, densities, need_owner, need_slot, near_index, near_coef
):
    width = positions.shape[1]
    blocks = lax.axis_size("blk")
    panels_all = blocks * width
    vmem = pl.BlockSpec(memory_space=pltpu.VMEM)
    params = pltpu.CompilerParams(vmem_limit_bytes=32 * 1024 * 1024)
    held, need = pl.pallas_call(
        pack_body,
        out_shape=(
            pltpu.VMEM((ROWS * width // LANES, LANES), jnp.float32),
            pltpu.VMEM((2, width), jnp.int32),
        ),
        in_specs=[vmem] * 6,
        out_specs=(vmem, vmem),
        name="pack",
    )(
        positions,
        normal_angles,
        areas.reshape(1, width),
        densities.reshape(2, width),
        need_owner.reshape(1, width),
        need_slot.reshape(1, width),
    )
    masks = []
    step = blocks // 2
    while step:
        masks.append(step | 1)
        step //= 2

    def trade(array, mask):
        return lax.ppermute(array, "blk", [(i, i ^ mask) for i in range(blocks)])

    def kernel(body, out_shape, operands, work, blocks_in, aliases=None):
        several = isinstance(out_shape, tuple)
        return pl.pallas_call(
            body,
            out_shape=out_shape,
            in_specs=[vmem] * len(operands),
            out_specs=(vmem,) * len(out_shape) if several else vmem,
            scratch_shapes=scratch(blocks_in, width),
            input_output_aliases=aliases or {},
            compiler_params=params,
            cost_estimate=far_cost(work, width),
            name="far",
        )(*operands)

    acc_shape = pltpu.VMEM((2, 2 * width, LANES), jnp.float32)
    tgt_shape = pltpu.VMEM((2 * width, FEATURES), jnp.bfloat16)
    gift_shape = pltpu.VMEM((ROWS, LANES), jnp.float32)
    own = latest = held
    early = mate = acc = tgt = gift = None
    count = 1
    for k, mask in enumerate(masks):
        early = held
        send = held if gift is None else jnp.concatenate([held, gift], 0)
        send, latest = lax.optimization_barrier((send, latest))
        arrived = trade(send, mask)
        if k == 0:
            acc, tgt, index, coef = pl.pallas_call(
                functools.partial(own_body, panels_all),
                out_shape=(
                    acc_shape,
                    tgt_shape,
                    pltpu.VMEM(near_index.shape, near_index.dtype),
                    pltpu.VMEM(near_coef.shape, near_coef.dtype),
                ),
                in_specs=[vmem, pl.BlockSpec(memory_space=pltpu.HBM), pl.BlockSpec(memory_space=pltpu.HBM)],
                out_specs=(vmem,) * 4,
                scratch_shapes=scratch(1, width) + [pltpu.SemaphoreType.DMA((2,))],
                compiler_params=params,
                cost_estimate=far_cost(1, width),
                name="far",
            )(
                own,
                pltpu.with_memory_space_constraint(near_index, pltpu.HBM),
                pltpu.with_memory_space_constraint(near_coef, pltpu.HBM),
            )
            own, acc = lax.optimization_barrier((own, acc))
            mate = trade(own, 1)
        elif k == 1:
            acc, tgt = kernel(
                functools.partial(mate_body, panels_all),
                (acc_shape, tgt_shape),
                (own, mate, latest, acc, tgt),
                3,
                2,
                {3: 0, 4: 1},
            )
        elif k < len(masks) - 1:
            final = k == len(masks) - 2
            out = kernel(
                functools.partial(both_body, panels_all, final),
                (acc_shape, gift_shape) if final else (acc_shape,),
                (latest, tgt, acc),
                count,
                count // 2,
                {2: 0},
            )
            acc = out[0]
            gift = out[1] if final else None
        else:
            acc = kernel(
                functools.partial(self_body, panels_all), acc_shape, (latest, tgt, acc), count // 2, count // 2, {2: 0}
            )
        arrived, acc = lax.optimization_barrier((arrived, acc))
        latest = arrived
        held = jnp.concatenate([held, arrived], 0)
        count *= 2
    out = kernel(
        functools.partial(last_body, panels_all, tuple(masks)),
        (jax.ShapeDtypeStruct(densities.shape, jnp.float32), acc_shape),
        (latest, tgt, acc, early, need, index, coef),
        count // 4,
        count // 4,
        {2: 1},
    )
    return out[0]


def solution(mesh):
    in_specs = (
        P(None, "blk"),
        P(None, "blk"),
        P("blk"),
        P("rhs", None, "blk"),
        P("blk", None),
        P("blk"),
        P(None, "blk"),
        P(None, None, "blk"),
    )
    out_specs = P("rhs", None, "blk")
    return jax.shard_map(
        on_device, mesh=mesh, in_specs=in_specs, out_specs=out_specs, check_vma=False
    )
```

```python
import functools
import math

import jax
import jax.numpy as jnp
from jax import lax
from jax.experimental import pallas as pl
from jax.experimental.pallas import tpu as pltpu
from jax.sharding import PartitionSpec as P

WAVE = 8.0
SOFT2 = 0.01
LANES = 128
ROWS = 8
KAPPA = WAVE / (2.0 * math.pi)
TURN = 0.5 / math.pi

SIN11 = (
    4.442883014678955,
    -7.308249473571777,
    3.6064748764038086,
    -0.8474637866020203,
    0.1160099749663353,
    -0.009900202974677086,
)
COS10 = (
    1.4142135381698608,
    -6.9788641929626465,
    5.73988151550293,
    -1.8882750272750854,
    0.3322519063949585,
    -0.03450220078229904,
)
ATAN = (
    0.15915492177009583,
    -0.05305047705769539,
    0.031808558851480484,
    -0.02253829687833786,
    0.016709592193365097,
    -0.011514633893966675,
    0.006331379525363445,
    -0.002292047953233123,
    0.00039099997957237065,
)


def horner(z, coefs):
    acc = coefs[-1]
    for c in coefs[-2::-1]:
        acc = acc * z + c
    return acc


def sincos_turns(turns):
    e = turns - jnp.round(turns)
    z = e * e
    s = e * horner(z, SIN11)
    c = horner(z, COS10)
    return s * c, 1.0 - s * s


def polar_turns(re, im):
    ax = jnp.abs(re)
    ay = jnp.abs(im)
    big = jnp.maximum(ax, ay)
    ratio = jnp.minimum(ax, ay) / jnp.where(big > 0.0, big, 1.0)
    z = ratio * ratio
    angle = ratio * horner(z, ATAN)
    angle = jnp.where(ay > ax, 0.25 - angle, angle)
    angle = jnp.where(re < 0.0, 0.5 - angle, angle)
    angle = jnp.where(im < 0.0, -angle, angle)
    return big * jnp.sqrt(1.0 + z), angle


def split3(x):
    x1 = x.astype(jnp.bfloat16).astype(jnp.float32)
    rest = x - x1
    x2 = rest.astype(jnp.bfloat16).astype(jnp.float32)
    return x1, x2, rest - x2


FEATURES = 24
CHUNK = 16
DEPTH = 2
UNROLL = 8
SIN5 = (2.0943219661712646, -1.5290753841400146, 0.32005560398101807)
TOP = 1.0 / SIN5[2]
SIN_A = SIN5[1] * TOP
SIN_B = SIN5[0] * TOP
TOP2 = TOP * TOP
MU = TOP2 * TOP / 4.0


def pack_body(pos_ref, ang_ref, area_ref, den_ref, owner_ref, slot_ref, out_ref, need_ref):
    need_ref[0:1, :] = owner_ref[...]
    need_ref[1:2, :] = slot_ref[...]
    for h in range(pos_ref.shape[1] // LANES):
        lanes = slice(h * LANES, (h + 1) * LANES)
        base = h * ROWS
        out_ref[base : base + 3, :] = pos_ref[:, lanes]
        out_ref[base + 3 : base + 5, :] = ang_ref[:, lanes]
        out_ref[base + 5 : base + 6, :] = area_ref[:, lanes]
        out_ref[base + 6 : base + 8, :] = den_ref[:, lanes]


def take_row(parts, halves, k):
    step = halves * ROWS
    rows = [
        jnp.concatenate(
            [
                ref[pl.ds(first * step + h * ROWS + k, count, stride=step if count > 1 else None), :]
                for h in range(halves)
            ],
            1,
        )
        for ref, first, count in parts
    ]
    return jnp.concatenate(rows, 0)


def source_features(panels_all, parts, feat, polar):
    blocks, width = polar.shape[0] // 2, polar.shape[1]
    halves = width // LANES

    def row(k):
        return take_row(parts, halves, k)

    x = [row(0), row(1), row(2)]
    sa, ca = sincos_turns(row(3) * (0.5 / math.pi))
    se, ce = sincos_turns(row(4) * (0.5 / math.pi))
    weight = row(5) * (KAPPA / MU / (4.0 * math.pi * math.sqrt(panels_all)))
    modulus, angle = polar_turns(row(6), row(7))
    modulus = modulus * weight
    polar[0:blocks, :] = modulus
    polar[blocks : 2 * blocks, :] = angle
    scaled = modulus * (WAVE * KAPPA)
    normal = [ca * ce * scaled, sa * ce * scaled, se * scaled]
    shift = -(x[0] * normal[0] + x[1] * normal[1] + x[2] * normal[2])
    norm2 = (x[0] * x[0] + x[1] * x[1] + x[2] * x[2]) * (KAPPA * KAPPA)

    def put(k, value):
        stride = halves * 2 * FEATURES if blocks > 1 else None
        for h in range(halves):
            feat[pl.ds(h * 2 * FEATURES + k, blocks, stride=stride), :] = value[
                :, h * LANES : (h + 1) * LANES
            ]

    for c in range(3):
        y1, y2, y3 = split3(x[c] * (-2.0 * KAPPA * KAPPA))
        m1, m2, m3 = split3(normal[c])
        for base, (v1, v2, v3) in ((0, (y1, y2, y3)), (FEATURES, (m1, m2, m3))):
            put(base + c, v1)
            put(base + 3 + c, v2)
            put(base + 6 + c, v3)
            put(base + 9 + c, v1)
            put(base + 12 + c, v2)
            put(base + 15 + c, v1)
    one = jnp.ones_like(weight)
    zero = jnp.zeros_like(weight)
    n1, n2, n3 = split3(norm2 + SOFT2 * KAPPA * KAPPA)
    s1, s2, s3 = split3(shift)
    for k, v in enumerate((one, one, one, n1, n2, n3)):
        put(18 + k, v)
    for k, v in enumerate((zero, zero, zero, s1, s2, s3)):
        put(FEATURES + 18 + k, v)


def target_features(g_ref, tgt, first):
    halves = tgt.shape[0] // 2 // LANES
    width = halves * LANES
    t = jnp.concatenate([g_ref[h * ROWS : h * ROWS + 3, :] for h in range(halves)], 1)
    t1, t2, t3 = split3(t)
    tt = t * t
    q1, q2, q3 = split3((tt[0:1] + tt[1:2] + tt[2:3]) * (KAPPA * KAPPA))
    ones3 = jnp.ones_like(t)
    stacked = jnp.concatenate([t1, t1, t1, t2, t2, t3, q1, q2, q3, ones3], 0)
    tgt[first : first + width, :] = stacked.T.astype(jnp.bfloat16)


def add_far(feat, polar, tgt, acc, first_block, count, top, bottom):
    blocks, width = polar.shape[0] // 2, polar.shape[1]
    halves = width // LANES

    def load_weights(b):
        base = b * (halves * 2 * FEATURES)
        return jnp.concatenate(
            [
                feat[pl.ds(pl.multiple_of(base + (h * 2 + j) * FEATURES, 8), FEATURES), :]
                for j in range(2)
                for h in range(halves)
            ],
            1,
        ).astype(jnp.bfloat16)

    def products(weights, rows):
        return jnp.dot(tgt[rows, :], weights, preferred_element_type=jnp.float32)

    def add_strip(mod_b, ang_b, res, rows):
        dist2 = res[:, :width]
        facing = res[:, width:]
        inv = lax.rsqrt(dist2)
        turns = dist2 * inv + ang_b
        e = turns - jnp.round(turns)
        z = e * e
        s = ((z + SIN_A) * z + SIN_B) * e
        q = s * s
        y = TOP2 - q
        c = (y * lax.rsqrt(y)) * (0.25 * TOP2 - q)
        s = s * (0.75 * TOP2 - q)
        double = facing * (inv * inv)
        b_part = double + inv * mod_b
        a_part = double * inv
        for part, value in enumerate((c * a_part, s * b_part, s * a_part, c * b_part)):
            total = acc[part, rows, :]
            for k in range(halves):
                total = total + value[:, k * LANES : (k + 1) * LANES]
            acc[part, rows, :] = total

    spans = [slice(r, r + CHUNK) for r in range(top, bottom, CHUNK)]
    unroll = math.gcd(count, UNROLL * width // (bottom - top))

    def add_block(b):
        weights = load_weights(b)
        mod_b = polar[pl.ds(b, 1), :]
        ang_b = polar[pl.ds(blocks + b, 1), :]
        ready = [products(weights, rows) for rows in spans[:DEPTH]]
        for k, rows in enumerate(spans):
            if k + DEPTH < len(spans):
                ready.append(products(weights, spans[k + DEPTH]))
            add_strip(mod_b, ang_b, ready[k], rows)

    if count == unroll:
        for u in range(count):
            add_block(first_block + u)
    else:

        @pl.loop(0, count // unroll)
        def _(group):
            for u in range(unroll):
                add_block(first_block + group * unroll + u)


def far_sums(acc, first, width):
    sums = ([], [])
    for h in range(first, first + width, LANES):
        ca, sb, sa, cb = (acc[k, h : h + LANES, :] for k in range(4))
        for part, total in enumerate((ca * TURN + sb, sa * TURN - cb)):
            sums[part].append(jnp.sum(total.T, 0, keepdims=True))
    return [jnp.concatenate(parts, 1) for parts in sums]


def own_body(panels_all, own_ref, index_in, coef_in, acc, tgt, index_out, coef_out, feat, polar, sems):
    width = polar.shape[1]
    copies = [
        pltpu.make_async_copy(index_in, index_out, sems.at[0]),
        pltpu.make_async_copy(coef_in, coef_out, sems.at[1]),
    ]
    for copy in copies:
        copy.start()
    target_features(own_ref, tgt, 0)
    source_features(panels_all, [(own_ref, 0, 1)], feat, polar)
    acc[...] = jnp.zeros_like(acc)
    add_far(feat, polar, tgt, acc, 0, 1, 0, width)
    for copy in copies:
        copy.wait()


def mate_body(panels_all, own_ref, mate_ref, g_ref, acc_in, tgt_in, acc, tgt, feat, polar):
    width = polar.shape[1]
    target_features(mate_ref, tgt, width)
    source_features(panels_all, [(own_ref, 0, 1), (g_ref, 0, 1)], feat, polar)
    add_far(feat, polar, tgt, acc, 0, 1, width, 2 * width)
    add_far(feat, polar, tgt, acc, 1, 1, 0, 2 * width)


def both_body(panels_all, final, g_ref, tgt, acc_in, acc, *rest):
    feat, polar = rest[-2:]
    blocks, width = polar.shape[0] // 2, polar.shape[1]
    source_features(panels_all, [(g_ref, 0, blocks)], feat, polar)
    add_far(feat, polar, tgt, acc, 0, blocks, 0, 2 * width)
    if final:
        gift = rest[0]
        gift[...] = jnp.zeros_like(gift)
        sums = far_sums(acc, width, width)
        for part in range(2):
            for h in range(width // LANES):
                k = part * (width // LANES) + h
                gift[k : k + 1, :] = sums[part][:, h * LANES : (h + 1) * LANES]


def self_body(panels_all, g_ref, tgt, acc_in, acc, feat, polar):
    blocks, width = polar.shape[0] // 2, polar.shape[1]
    source_features(panels_all, [(g_ref, 0, blocks)], feat, polar)
    add_far(feat, polar, tgt, acc, 0, blocks, 0, width)


def last_body(
    panels_all, masks, g_ref, tgt, acc_in, early_ref, need_ref, index_ref, coef_ref, out_ref, acc, feat, polar
):
    width = need_ref.shape[1]
    halves = width // LANES
    me = lax.axis_index("blk")
    fresh = polar.shape[0] // 2
    held = 2 * fresh
    source_features(panels_all, [(g_ref, fresh, fresh)], feat, polar)
    add_far(feat, polar, tgt, acc, 0, fresh, 0, width)
    far = far_sums(acc, 0, width)

    owner = need_ref[0:1, :]
    slot = need_ref[1:2, :]
    blocks = 2 * held
    den = []
    for k in (6, 7):
        den.append(take_row([(early_ref, 0, held), (g_ref, 0, held)], halves, k))
    need = []
    for h in range(halves):
        lanes = slice(h * LANES, (h + 1) * LANES)
        slot_h = jnp.broadcast_to(slot[:, lanes], (ROWS, LANES))
        own_h = jnp.broadcast_to(owner[:, lanes], (ROWS, LANES))
        sums = [jnp.zeros((ROWS, LANES), jnp.float32)] * 2
        for p in range(0, blocks, ROWS):
            place = lax.broadcasted_iota(jnp.int32, (ROWS, LANES), 0) + p
            device = me
            for k, mask in enumerate(masks):
                device = device ^ (((place >> k) & 1) * mask)
            mine = own_h == device
            for part in range(2):
                for k in range(halves):
                    got = jnp.take_along_axis(
                        den[part][p : p + ROWS, k * LANES : (k + 1) * LANES], slot_h % LANES, axis=1
                    )
                    sums[part] = sums[part] + jnp.where(mine & (slot_h // LANES == k), got, 0.0)
        need.append([jnp.broadcast_to(jnp.sum(v, 0, keepdims=True), (ROWS, LANES)) for v in sums])

    count = index_ref.shape[0]
    for h in range(halves):
        lanes = slice(h * LANES, (h + 1) * LANES)
        near = [jnp.zeros((ROWS, LANES), jnp.float32)] * 2
        for m in range(0, count, ROWS):
            where = index_ref[m : m + ROWS, lanes]
            picked = []
            for part in range(2):
                got = jnp.zeros((ROWS, LANES), jnp.float32)
                for k in range(halves):
                    one_half = jnp.take_along_axis(need[k][part], where % LANES, axis=1)
                    got = jnp.where(where // LANES == k, one_half, got)
                picked.append(got)
            cr = coef_ref[0, m : m + ROWS, lanes]
            ci = coef_ref[1, m : m + ROWS, lanes]
            near[0] = near[0] + (cr * picked[0] - ci * picked[1])
            near[1] = near[1] + (cr * picked[1] + ci * picked[0])
        for part in range(2):
            own = early_ref[h * ROWS + 6 + part : h * ROWS + 7 + part, :]
            k = blocks * halves * ROWS // 2 + part * halves + h
            gift = g_ref[k : k + 1, :]
            out_ref[0, part : part + 1, lanes] = (
                0.5 * own + (far[part][:, lanes] + gift) + jnp.sum(near[part], 0, keepdims=True)
            )


def scratch(blocks, width):
    return [
        pltpu.VMEM((blocks * 2 * FEATURES * width // LANES, LANES), jnp.float32),
        pltpu.VMEM((2 * blocks, width), jnp.float32),
    ]


def far_cost(blocks, width):
    return pl.CostEstimate(
        flops=60 * blocks * width * width, bytes_accessed=0, transcendentals=2 * blocks * width * width
    )


def on_device(
    positions, normal_angles, areas, densities, need_owner, need_slot, near_index, near_coef
):
    width = positions.shape[1]
    blocks = lax.axis_size("blk")
    panels_all = blocks * width
    vmem = pl.BlockSpec(memory_space=pltpu.VMEM)
    params = pltpu.CompilerParams(vmem_limit_bytes=32 * 1024 * 1024)
    held, need = pl.pallas_call(
        pack_body,
        out_shape=(
            pltpu.VMEM((ROWS * width // LANES, LANES), jnp.float32),
            pltpu.VMEM((2, width), jnp.int32),
        ),
        in_specs=[vmem] * 6,
        out_specs=(vmem, vmem),
        name="pack",
    )(
        positions,
        normal_angles,
        areas.reshape(1, width),
        densities.reshape(2, width),
        need_owner.reshape(1, width),
        need_slot.reshape(1, width),
    )
    masks = []
    step = blocks // 2
    while step:
        masks.append(step | 1)
        step //= 2

    def trade(array, mask):
        return lax.ppermute(array, "blk", [(i, i ^ mask) for i in range(blocks)])

    def kernel(body, out_shape, operands, work, blocks_in, aliases=None):
        several = isinstance(out_shape, tuple)
        return pl.pallas_call(
            body,
            out_shape=out_shape,
            in_specs=[vmem] * len(operands),
            out_specs=(vmem,) * len(out_shape) if several else vmem,
            scratch_shapes=scratch(blocks_in, width),
            input_output_aliases=aliases or {},
            compiler_params=params,
            cost_estimate=far_cost(work, width),
            name="far",
        )(*operands)

    acc_shape = pltpu.VMEM((4, 2 * width, LANES), jnp.float32)
    tgt_shape = pltpu.VMEM((2 * width, FEATURES), jnp.bfloat16)
    gift_shape = pltpu.VMEM((ROWS, LANES), jnp.float32)
    own = latest = held
    early = mate = acc = tgt = gift = None
    count = 1
    for k, mask in enumerate(masks):
        early = held
        send = held if gift is None else jnp.concatenate([held, gift], 0)
        send, latest = lax.optimization_barrier((send, latest))
        arrived = trade(send, mask)
        if k == 0:
            acc, tgt, index, coef = pl.pallas_call(
                functools.partial(own_body, panels_all),
                out_shape=(
                    acc_shape,
                    tgt_shape,
                    pltpu.VMEM(near_index.shape, near_index.dtype),
                    pltpu.VMEM(near_coef.shape, near_coef.dtype),
                ),
                in_specs=[vmem, pl.BlockSpec(memory_space=pltpu.HBM), pl.BlockSpec(memory_space=pltpu.HBM)],
                out_specs=(vmem,) * 4,
                scratch_shapes=scratch(1, width) + [pltpu.SemaphoreType.DMA((2,))],
                compiler_params=params,
                cost_estimate=far_cost(1, width),
                name="far",
            )(
                own,
                pltpu.with_memory_space_constraint(near_index, pltpu.HBM),
                pltpu.with_memory_space_constraint(near_coef, pltpu.HBM),
            )
            own, acc = lax.optimization_barrier((own, acc))
            mate = trade(own, 1)
        elif k == 1:
            acc, tgt = kernel(
                functools.partial(mate_body, panels_all),
                (acc_shape, tgt_shape),
                (own, mate, latest, acc, tgt),
                3,
                2,
                {3: 0, 4: 1},
            )
        elif k < len(masks) - 1:
            final = k == len(masks) - 2
            out = kernel(
                functools.partial(both_body, panels_all, final),
                (acc_shape, gift_shape) if final else (acc_shape,),
                (latest, tgt, acc),
                count,
                count // 2,
                {2: 0},
            )
            acc = out[0]
            gift = out[1] if final else None
        else:
            acc = kernel(
                functools.partial(self_body, panels_all), acc_shape, (latest, tgt, acc), count // 2, count // 2, {2: 0}
            )
        arrived, acc = lax.optimization_barrier((arrived, acc))
        latest = arrived
        held = jnp.concatenate([held, arrived], 0)
        count *= 2
    out = kernel(
        functools.partial(last_body, panels_all, tuple(masks)),
        (jax.ShapeDtypeStruct(densities.shape, jnp.float32), acc_shape),
        (latest, tgt, acc, early, need, index, coef),
        count // 4,
        count // 4,
        {2: 1},
    )
    return out[0]


def solution(mesh):
    in_specs = (
        P(None, "blk"),
        P(None, "blk"),
        P("blk"),
        P("rhs", None, "blk"),
        P("blk", None),
        P("blk"),
        P(None, "blk"),
        P(None, None, "blk"),
    )
    out_specs = P("rhs", None, "blk")
    return jax.shard_map(
        on_device, mesh=mesh, in_specs=in_specs, out_specs=out_specs, check_vma=False
    )
```

```python
import functools
import math

import jax
import jax.numpy as jnp
from jax import lax
from jax.experimental import pallas as pl
from jax.experimental.pallas import tpu as pltpu
from jax.sharding import PartitionSpec as P

WAVE = 8.0
SOFT2 = 0.01
LANES = 128
ROWS = 8
KAPPA = WAVE / (2.0 * math.pi)

SIN11 = (
    4.442883014678955,
    -7.308249473571777,
    3.6064748764038086,
    -0.8474637866020203,
    0.1160099749663353,
    -0.009900202974677086,
)
COS10 = (
    1.4142135381698608,
    -6.9788641929626465,
    5.73988151550293,
    -1.8882750272750854,
    0.3322519063949585,
    -0.03450220078229904,
)
ATAN = (
    0.15915492177009583,
    -0.05305047705769539,
    0.031808558851480484,
    -0.02253829687833786,
    0.016709592193365097,
    -0.011514633893966675,
    0.006331379525363445,
    -0.002292047953233123,
    0.00039099997957237065,
)


def horner(z, coefs):
    acc = coefs[-1]
    for c in coefs[-2::-1]:
        acc = acc * z + c
    return acc


def sincos_turns(turns):
    e = turns - jnp.round(turns)
    z = e * e
    s = e * horner(z, SIN11)
    c = horner(z, COS10)
    return s * c, 1.0 - s * s


def polar_turns(re, im):
    ax = jnp.abs(re)
    ay = jnp.abs(im)
    big = jnp.maximum(ax, ay)
    ratio = jnp.minimum(ax, ay) / jnp.where(big > 0.0, big, 1.0)
    z = ratio * ratio
    angle = ratio * horner(z, ATAN)
    angle = jnp.where(ay > ax, 0.25 - angle, angle)
    angle = jnp.where(re < 0.0, 0.5 - angle, angle)
    angle = jnp.where(im < 0.0, -angle, angle)
    return big * jnp.sqrt(1.0 + z), angle


def split3(x):
    x1 = x.astype(jnp.bfloat16).astype(jnp.float32)
    rest = x - x1
    x2 = rest.astype(jnp.bfloat16).astype(jnp.float32)
    return x1, x2, rest - x2


FEATURES = 24
CHUNK = 16
DEPTH = 2
UNROLL = 8
SIN5 = (2.0943219661712646, -1.5290753841400146, 0.32005560398101807)
TOP = 1.0 / SIN5[2]
SIN_A = SIN5[1] * TOP
SIN_B = SIN5[0] * TOP
TOP2 = TOP * TOP
MU = TOP2 * TOP / 4.0


def pack_body(pos_ref, ang_ref, area_ref, den_ref, owner_ref, slot_ref, out_ref, need_ref):
    need_ref[0:1, :] = owner_ref[...]
    need_ref[1:2, :] = slot_ref[...]
    for h in range(pos_ref.shape[1] // LANES):
        lanes = slice(h * LANES, (h + 1) * LANES)
        base = h * ROWS
        out_ref[base : base + 3, :] = pos_ref[:, lanes]
        out_ref[base + 3 : base + 5, :] = ang_ref[:, lanes]
        out_ref[base + 5 : base + 6, :] = area_ref[:, lanes]
        out_ref[base + 6 : base + 8, :] = den_ref[:, lanes]


def take_row(parts, halves, k):
    step = halves * ROWS
    rows = [
        jnp.concatenate(
            [
                ref[pl.ds(first * step + h * ROWS + k, count, stride=step if count > 1 else None), :]
                for h in range(halves)
            ],
            1,
        )
        for ref, first, count in parts
    ]
    return jnp.concatenate(rows, 0)


def source_features(panels_all, parts, feat, polar):
    blocks, width = polar.shape[0] // 2, polar.shape[1]
    halves = width // LANES

    def row(k):
        return take_row(parts, halves, k)

    x = [row(0), row(1), row(2)]
    sa, ca = sincos_turns(row(3) * (0.5 / math.pi))
    se, ce = sincos_turns(row(4) * (0.5 / math.pi))
    weight = row(5) * (KAPPA / MU / (4.0 * math.pi * math.sqrt(panels_all)))
    modulus, angle = polar_turns(row(6), row(7))
    modulus = modulus * weight
    polar[0:blocks, :] = modulus
    polar[blocks : 2 * blocks, :] = angle
    scaled = modulus * (WAVE * KAPPA)
    normal = [ca * ce * scaled, sa * ce * scaled, se * scaled]
    shift = -(x[0] * normal[0] + x[1] * normal[1] + x[2] * normal[2])
    norm2 = (x[0] * x[0] + x[1] * x[1] + x[2] * x[2]) * (KAPPA * KAPPA)

    def put(k, value):
        stride = halves * 2 * FEATURES if blocks > 1 else None
        for h in range(halves):
            feat[pl.ds(h * 2 * FEATURES + k, blocks, stride=stride), :] = value[
                :, h * LANES : (h + 1) * LANES
            ]

    for c in range(3):
        y1, y2, y3 = split3(x[c] * (-2.0 * KAPPA * KAPPA))
        m1, m2, m3 = split3(normal[c])
        for base, (v1, v2, v3) in ((0, (y1, y2, y3)), (FEATURES, (m1, m2, m3))):
            put(base + c, v1)
            put(base + 3 + c, v2)
            put(base + 6 + c, v3)
            put(base + 9 + c, v1)
            put(base + 12 + c, v2)
            put(base + 15 + c, v1)
    one = jnp.ones_like(weight)
    zero = jnp.zeros_like(weight)
    n1, n2, n3 = split3(norm2 + SOFT2 * KAPPA * KAPPA)
    s1, s2, s3 = split3(shift)
    for k, v in enumerate((one, one, one, n1, n2, n3)):
        put(18 + k, v)
    for k, v in enumerate((zero, zero, zero, s1, s2, s3)):
        put(FEATURES + 18 + k, v)


def target_features(g_ref, tgt, first):
    halves = tgt.shape[0] // 2 // LANES
    width = halves * LANES
    t = jnp.concatenate([g_ref[h * ROWS : h * ROWS + 3, :] for h in range(halves)], 1)
    t1, t2, t3 = split3(t)
    tt = t * t
    q1, q2, q3 = split3((tt[0:1] + tt[1:2] + tt[2:3]) * (KAPPA * KAPPA))
    ones3 = jnp.ones_like(t)
    stacked = jnp.concatenate([t1, t1, t1, t2, t2, t3, q1, q2, q3, ones3], 0)
    tgt[first : first + width, :] = stacked.T.astype(jnp.bfloat16)


def add_far(feat, polar, tgt, acc, first_block, count, top, bottom, side=None):
    blocks, width = polar.shape[0] // 2, polar.shape[1]
    halves = width // LANES

    def load_weights(b):
        base = b * (halves * 2 * FEATURES)
        return jnp.concatenate(
            [
                feat[pl.ds(pl.multiple_of(base + (h * 2 + j) * FEATURES, 8), FEATURES), :]
                for j in range(2)
                for h in range(halves)
            ],
            1,
        ).astype(jnp.bfloat16)

    def products(weights, rows):
        return jnp.dot(tgt[rows, :], weights, preferred_element_type=jnp.float32)

    def add_strip(mod_b, ang_b, res, rows):
        dist2 = res[:, :width]
        facing = res[:, width:]
        inv = lax.rsqrt(dist2)
        turns = dist2 * inv + ang_b
        e = turns - jnp.round(turns)
        z = e * e
        s = ((z + SIN_A) * z + SIN_B) * e
        q = s * s
        y = TOP2 - q
        c = (y * lax.rsqrt(y)) * (0.25 * TOP2 - q)
        s = s * (0.75 * TOP2 - q)
        double = facing * (inv * inv)
        b_part = double + inv * mod_b
        a_part = double * (inv * (0.5 / math.pi))
        re = c * a_part + s * b_part
        im = s * a_part - c * b_part
        for part, value in ((0, re), (1, im)):
            total = acc[part, rows, :]
            for k in range(halves):
                total = total + value[:, k * LANES : (k + 1) * LANES]
            acc[part, rows, :] = total

    spans = [slice(r, r + CHUNK) for r in range(top, bottom, CHUNK)]
    unroll = math.gcd(count, UNROLL * width // (bottom - top))

    def add_block(b):
        weights = load_weights(b)
        mod_b = polar[pl.ds(b, 1), :]
        ang_b = polar[pl.ds(blocks + b, 1), :]
        ready = [products(weights, rows) for rows in spans[:DEPTH]]
        for k, rows in enumerate(spans):
            if k + DEPTH < len(spans):
                ready.append(products(weights, spans[k + DEPTH]))
            add_strip(mod_b, ang_b, ready[k], rows)
            if side is not None and count == unroll:
                next(side, None)

    if count == unroll:
        for u in range(count):
            add_block(first_block + u)
    else:

        @pl.loop(0, count // unroll)
        def _(group):
            for u in range(unroll):
                add_block(first_block + group * unroll + u)


def far_sums(acc, first, width):
    return [
        jnp.concatenate(
            [
                jnp.sum(acc[part, h : h + LANES, :].T, 0, keepdims=True)
                for h in range(first, first + width, LANES)
            ],
            1,
        )
        for part in range(2)
    ]


def own_body(panels_all, own_ref, index_in, coef_in, acc, tgt, index_out, coef_out, feat, polar, sems):
    width = polar.shape[1]
    copies = [
        pltpu.make_async_copy(index_in, index_out, sems.at[0]),
        pltpu.make_async_copy(coef_in, coef_out, sems.at[1]),
    ]
    for copy in copies:
        copy.start()
    target_features(own_ref, tgt, 0)
    source_features(panels_all, [(own_ref, 0, 1)], feat, polar)
    acc[...] = jnp.zeros_like(acc)
    add_far(feat, polar, tgt, acc, 0, 1, 0, width)
    for copy in copies:
        copy.wait()


def mate_body(panels_all, own_ref, mate_ref, g_ref, acc_in, tgt_in, acc, tgt, feat, polar):
    width = polar.shape[1]
    target_features(mate_ref, tgt, width)
    source_features(panels_all, [(own_ref, 0, 1), (g_ref, 0, 1)], feat, polar)
    add_far(feat, polar, tgt, acc, 0, 1, width, 2 * width)
    add_far(feat, polar, tgt, acc, 1, 1, 0, 2 * width)


def both_body(panels_all, final, g_ref, tgt, acc_in, acc, *rest):
    feat, polar = rest[-2:]
    blocks, width = polar.shape[0] // 2, polar.shape[1]
    source_features(panels_all, [(g_ref, 0, blocks)], feat, polar)
    add_far(feat, polar, tgt, acc, 0, blocks, 0, 2 * width)
    if final:
        gift = rest[0]
        gift[...] = jnp.zeros_like(gift)
        sums = far_sums(acc, width, width)
        for part in range(2):
            for h in range(width // LANES):
                k = part * (width // LANES) + h
                gift[k : k + 1, :] = sums[part][:, h * LANES : (h + 1) * LANES]


def self_body(panels_all, g_ref, tgt, acc_in, acc, feat, polar):
    blocks, width = polar.shape[0] // 2, polar.shape[1]
    source_features(panels_all, [(g_ref, 0, blocks)], feat, polar)
    add_far(feat, polar, tgt, acc, 0, blocks, 0, width)


def last_body(
    panels_all, masks, g_ref, tgt, acc_in, early_ref, need_ref, index_ref, coef_ref, out_ref, feat, polar, acc
):
    width = need_ref.shape[1]
    halves = width // LANES
    me = lax.axis_index("blk")
    fresh = polar.shape[0] // 2
    held = 2 * fresh
    acc[...] = acc_in[:, :width, :]
    blocks = 2 * held
    source_features(panels_all, [(g_ref, fresh, fresh)], feat, polar)
    result = []

    def near_field():
        owner = need_ref[0:1, :]
        slot = need_ref[1:2, :]
        den = []
        for k in (6, 7):
            den.append(take_row([(early_ref, 0, held), (g_ref, 0, held)], halves, k))
        need = []
        for h in range(halves):
            lanes = slice(h * LANES, (h + 1) * LANES)
            slot_h = jnp.broadcast_to(slot[:, lanes], (ROWS, LANES))
            own_h = jnp.broadcast_to(owner[:, lanes], (ROWS, LANES))
            sums = [jnp.zeros((ROWS, LANES), jnp.float32)] * 2
            for p in range(0, blocks, ROWS):
                place = lax.broadcasted_iota(jnp.int32, (ROWS, LANES), 0) + p
                device = me
                for k, mask in enumerate(masks):
                    device = device ^ (((place >> k) & 1) * mask)
                mine = own_h == device
                for part in range(2):
                    for k in range(halves):
                        got = jnp.take_along_axis(
                            den[part][p : p + ROWS, k * LANES : (k + 1) * LANES], slot_h % LANES, axis=1
                        )
                        sums[part] = sums[part] + jnp.where(mine & (slot_h // LANES == k), got, 0.0)
                    yield
            need.append([jnp.broadcast_to(jnp.sum(v, 0, keepdims=True), (ROWS, LANES)) for v in sums])

        count = index_ref.shape[0]
        for h in range(halves):
            lanes = slice(h * LANES, (h + 1) * LANES)
            near = [jnp.zeros((ROWS, LANES), jnp.float32)] * 2
            for m in range(0, count, ROWS):
                where = index_ref[m : m + ROWS, lanes]
                picked = []
                for part in range(2):
                    got = jnp.zeros((ROWS, LANES), jnp.float32)
                    for k in range(halves):
                        one_half = jnp.take_along_axis(need[k][part], where % LANES, axis=1)
                        got = jnp.where(where // LANES == k, one_half, got)
                    picked.append(got)
                    yield
                cr = coef_ref[0, m : m + ROWS, lanes]
                ci = coef_ref[1, m : m + ROWS, lanes]
                near[0] = near[0] + (cr * picked[0] - ci * picked[1])
                near[1] = near[1] + (cr * picked[1] + ci * picked[0])
            result.append([jnp.sum(v, 0, keepdims=True) for v in near])
            yield

    far = []

    def side_work():
        laid = 0
        for _ in near_field():
            laid += 1
            yield
        for _ in range(laid, ((fresh - 1) * width + LANES) // CHUNK):
            yield
        far.append(far_sums(acc, 0, LANES))
        yield

    side = side_work()
    add_far(feat, polar, tgt, acc, 0, fresh, 0, width, side)
    for _ in side:
        pass
    far += [far_sums(acc, h * LANES, LANES) for h in range(1, halves)]
    for h in range(halves):
        lanes = slice(h * LANES, (h + 1) * LANES)
        for part in range(2):
            own = early_ref[h * ROWS + 6 + part : h * ROWS + 7 + part, :]
            k = blocks * halves * ROWS // 2 + part * halves + h
            gift = g_ref[k : k + 1, :]
            out_ref[0, part : part + 1, lanes] = (
                0.5 * own + (far[h][part] + gift) + result[h][part]
            )


def scratch(blocks, width):
    return [
        pltpu.VMEM((blocks * 2 * FEATURES * width // LANES, LANES), jnp.float32),
        pltpu.VMEM((2 * blocks, width), jnp.float32),
    ]


def far_cost(blocks, width):
    return pl.CostEstimate(
        flops=60 * blocks * width * width, bytes_accessed=0, transcendentals=2 * blocks * width * width
    )


def on_device(
    positions, normal_angles, areas, densities, need_owner, need_slot, near_index, near_coef
):
    width = positions.shape[1]
    blocks = lax.axis_size("blk")
    panels_all = blocks * width
    vmem = pl.BlockSpec(memory_space=pltpu.VMEM)
    params = pltpu.CompilerParams(vmem_limit_bytes=32 * 1024 * 1024)
    held, need = pl.pallas_call(
        pack_body,
        out_shape=(
            pltpu.VMEM((ROWS * width // LANES, LANES), jnp.float32),
            pltpu.VMEM((2, width), jnp.int32),
        ),
        in_specs=[vmem] * 6,
        out_specs=(vmem, vmem),
        name="pack",
    )(
        positions,
        normal_angles,
        areas.reshape(1, width),
        densities.reshape(2, width),
        need_owner.reshape(1, width),
        need_slot.reshape(1, width),
    )
    masks = []
    step = blocks // 2
    while step:
        masks.append(step | 1)
        step //= 2

    def trade(array, mask):
        return lax.ppermute(array, "blk", [(i, i ^ mask) for i in range(blocks)])

    def kernel(body, out_shape, operands, work, blocks_in, aliases=None):
        several = isinstance(out_shape, tuple)
        return pl.pallas_call(
            body,
            out_shape=out_shape,
            in_specs=[vmem] * len(operands),
            out_specs=(vmem,) * len(out_shape) if several else vmem,
            scratch_shapes=scratch(blocks_in, width),
            input_output_aliases=aliases or {},
            compiler_params=params,
            cost_estimate=far_cost(work, width),
            name="far",
        )(*operands)

    acc_shape = pltpu.VMEM((2, 2 * width, LANES), jnp.float32)
    tgt_shape = pltpu.VMEM((2 * width, FEATURES), jnp.bfloat16)
    gift_shape = pltpu.VMEM((ROWS, LANES), jnp.float32)
    own = latest = held
    early = mate = acc = tgt = gift = None
    count = 1
    for k, mask in enumerate(masks):
        early = held
        send = held if gift is None else jnp.concatenate([held, gift], 0)
        send, latest = lax.optimization_barrier((send, latest))
        arrived = trade(send, mask)
        if k == 0:
            acc, tgt, index, coef = pl.pallas_call(
                functools.partial(own_body, panels_all),
                out_shape=(
                    acc_shape,
                    tgt_shape,
                    pltpu.VMEM(near_index.shape, near_index.dtype),
                    pltpu.VMEM(near_coef.shape, near_coef.dtype),
                ),
                in_specs=[vmem, pl.BlockSpec(memory_space=pltpu.HBM), pl.BlockSpec(memory_space=pltpu.HBM)],
                out_specs=(vmem,) * 4,
                scratch_shapes=scratch(1, width) + [pltpu.SemaphoreType.DMA((2,))],
                compiler_params=params,
                cost_estimate=far_cost(1, width),
                name="far",
            )(
                own,
                pltpu.with_memory_space_constraint(near_index, pltpu.HBM),
                pltpu.with_memory_space_constraint(near_coef, pltpu.HBM),
            )
            own, acc = lax.optimization_barrier((own, acc))
            mate = trade(own, 1)
        elif k == 1:
            acc, tgt = kernel(
                functools.partial(mate_body, panels_all),
                (acc_shape, tgt_shape),
                (own, mate, latest, acc, tgt),
                3,
                2,
                {3: 0, 4: 1},
            )
        elif k < len(masks) - 1:
            final = k == len(masks) - 2
            out = kernel(
                functools.partial(both_body, panels_all, final),
                (acc_shape, gift_shape) if final else (acc_shape,),
                (latest, tgt, acc),
                count,
                count // 2,
                {2: 0},
            )
            acc = out[0]
            gift = out[1] if final else None
        else:
            acc = kernel(
                functools.partial(self_body, panels_all), acc_shape, (latest, tgt, acc), count // 2, count // 2, {2: 0}
            )
        arrived, acc = lax.optimization_barrier((arrived, acc))
        latest = arrived
        held = jnp.concatenate([held, arrived], 0)
        count *= 2
    return pl.pallas_call(
        functools.partial(last_body, panels_all, tuple(masks)),
        out_shape=jax.ShapeDtypeStruct(densities.shape, jnp.float32),
        in_specs=[vmem] * 7,
        out_specs=vmem,
        scratch_shapes=scratch(count // 4, width) + [pltpu.VMEM((2, width, LANES), jnp.float32)],
        compiler_params=params,
        cost_estimate=far_cost(count // 4, width),
        name="last",
    )(latest, tgt, acc, early, need, index, coef)


def solution(mesh):
    in_specs = (
        P(None, "blk"),
        P(None, "blk"),
        P("blk"),
        P("rhs", None, "blk"),
        P("blk", None),
        P("blk"),
        P(None, "blk"),
        P(None, None, "blk"),
    )
    out_specs = P("rhs", None, "blk")
    return jax.shard_map(
        on_device, mesh=mesh, in_specs=in_specs, out_specs=out_specs, check_vma=False
    )
```
